32 devices in a mesh: px: 8 (over y, x, core), py: 4 (over z).
Axes of the slice: x: 2, y: 2, z: 4, core: 2. Of those that a mesh axis runs over, the one named last changes fastest.
Arguments:
- fields: bfloat16 [4, 16, 1024, 1024], P(None, None, 'px', 'py'), may hold values from -6 to 6
- x_operators: bfloat16 [3, 1024, 1024], replicated
- y_operators: bfloat16 [3, 1024, 1024], replicated
- viscosity: float32 [4], replicated, may hold values from 0.1 to 1
- wall_tile: int32 [4096], P(('px', 'py')), may hold values from 0 to 2047
- wall_owner: int32 [4096, 1], P(('px', 'py')), may hold values from 0 to 31; in each aligned block of 128 rows (0 to 127, 128 to 255, ...) at most 16 rows name the same one
- wall_row: int32 [4096], P(('px', 'py')), may hold values from 0 to 63
- solid_temp: float32 [512, 1024], P('px', 'py'), may hold values from -6 to 6
- conductivity: float32 [512, 1024], P('px', 'py'), may hold values from 0.2 to 1
Outputs:
- new_fields: bfloat16 [4, 16, 1024, 1024], P(None, None, 'px', 'py')
- new_solid: float32 [512, 1024], P('px', 'py')
The draws below stay inside these ranges and needn't reach their ends.
Inputs may be any that keep to these rules, and one draw needn't show every extreme that they name: `wall_owner`: at most 16 of one device's wall slots name the same owner, and some owner receives exactly 16 of them. `wall_tile`: A y-line of the sending device's own block, numbered z times its x cells plus its local x.
All inputs are finite; a program needn't handle non-finite values.
Results may differ from the reference program's by a relative error of at most 0.0054.
Values may be sent and summed in bfloat16 or wider, within the bound.
No kernel may reach another device: no remote copies, remote signals or barrier semaphores. Data moves between devices by JAX's collectives and lax.ppermute only.
A program may use at most 128 MiB of HBM per device.

```python
import math
import jax
import jax.numpy as jnp
import numpy as np
from jax import lax

FIELDS = 4
NX = 1024
NY = 1024
NZ = 16
SR = 64
WALL_DEV = 128
COND_STEPS = 8
CAP = 16
SOLID_ROWS = 512
N_PX = 8
N_PY = 4
DEVICES = 32


def operator_stack(key, width):
    first, second = jax.random.split(key, 2)
    noise = jax.random.normal(first, (3, width, width), jnp.float32) * 0.6 / jnp.sqrt(width * 1.0)
    diagonal = jax.random.uniform(second, (3, width), jnp.float32, 0.6, 1.4)
    matrix = noise + jnp.eye(width, dtype=jnp.float32)[None, :, :] * diagonal[:, :, None]
    return matrix.astype(jnp.bfloat16)


def draw_x_operators(key, part):
    return operator_stack(jax.random.fold_in(key, 11), NX)


def draw_y_operators(key, part):
    return operator_stack(jax.random.fold_in(key, 23), NY)


def with_ends(drawn, rng, least, top_value):
    spot = [jax.random.randint(jax.random.fold_in(rng, axis), (), 0, length) for axis, length in enumerate(drawn.shape)]
    main_axis = drawn.shape.index(max(drawn.shape))
    beside = spot[:main_axis] + [(spot[main_axis] + 1) % drawn.shape[main_axis]] + spot[main_axis + 1:]
    return drawn.at[tuple(spot)].set(least).at[tuple(beside)].set(top_value)


def steps_of(own_key, dims, cuts, smallest, top_value):
    def one(axis_at, shards_of):
        heights = jax.random.uniform(jax.random.fold_in(jax.random.fold_in(own_key, 6), axis_at), (shards_of,), jnp.float32, smallest / len(cuts), top_value / len(cuts))
        return jnp.repeat(jnp.exp(heights), dims[axis_at] // shards_of).reshape((-1,) + (1,) * (len(dims) - axis_at - 1))

    factor_of = one(*cuts[0])
    for cut in cuts[1:]:
        factor_of = factor_of * one(*cut)
    return factor_of


def assign_block(key, own, number, rows, amount, top, most, skew):
    order = jax.random.permutation(key, amount)
    packed, common = load_shares(amount, rows * top, most, skew, True), load_shares(amount, rows * top, most, skew, False)
    places = jnp.arange(amount)

    def named(lengths, rotation):
        used = int((lengths > 0).sum())
        fixed = max(1, used // 4)
        passed = fixed + (places - fixed + rotation * (used - fixed)) % max(1, amount - fixed)
        return jnp.zeros((amount,), jnp.int32).at[order[jnp.where(places < fixed, places, passed)]].set(jnp.asarray(lengths, jnp.int32))

    lengths = jnp.where(number % 4 == 0, named(packed, number // 4), named(common, number - number // 4 - 1))
    mixed = jax.random.permutation(jax.random.fold_in(own, 3), amount)
    donor, sink = mixed[0:amount // 2 * 2:2], mixed[1:amount // 2 * 2:2]
    margin = jnp.minimum(lengths[donor] - 1, most - lengths[sink]) // 2
    margin = jnp.where((donor == order[0]) | (sink == order[0]) | (lengths[sink] == 0), 0, jnp.maximum(margin, 0))
    passed = jax.random.randint(jax.random.fold_in(own, 4), (amount // 2,), 0, 1 << 20) % (margin + 1)
    lengths = lengths.at[donor].add(-passed).at[sink].add(passed)
    labels = jnp.searchsorted(jnp.cumsum(lengths), jnp.arange(rows * top), side="right").astype(jnp.int32)
    table = labels.reshape(top, rows).T
    table = table[jax.random.permutation(jax.random.fold_in(own, 1), rows)]
    rotation = jax.random.randint(jax.random.fold_in(own, 2), (rows, 1), 0, top)
    return jnp.take_along_axis(table, (jnp.arange(top)[None, :] + rotation) % top, axis=1)


def load_shares(count, total, limit, slope, full):
    loads = [(1 << 20) // math.isqrt(standing ** slope) + 1 for standing in range(1, count + 1)]
    largest = limit if full else min(limit, max(-(-total // count), total * loads[0] // sum(loads)))
    least = 1 if total - largest >= count - 1 else 0
    counts, surplus = [largest] + [least] * (count - 1), total - largest - least * (count - 1)
    while surplus > 0:
        movable = [i for i in range(1, count) if counts[i] < largest] or [i for i in range(1, count) if counts[i] < limit]
        mass, remaining = sum([loads[i] for i in movable]), surplus
        for i in movable:
            addition = min(limit - counts[i], max(1, remaining * loads[i] // mass), surplus)
            counts[i] = counts[i] + addition
            surplus = surplus - addition
    return np.array(counts)


def gaussian(rng, shape, scale, reach, cuts=(), held_as=jnp.bfloat16):
    drawn = jax.random.normal(rng, shape, jnp.float32) * scale
    if len(cuts) > 0:
        drawn = steps_of(rng, shape, cuts, -0.22, 0.18) * drawn
    return jnp.clip(drawn, min=-reach, max=reach).astype(held_as)


def setup_inputs(seed: int = 0) -> dict:
    keys = jax.random.split(jax.random.key(seed), 10)
    fields = gaussian(keys[0], (FIELDS, NZ, NX, NY), 1.0, 6.0, ((2, 8), (3, 4)))
    x_operators = draw_x_operators(jax.random.fold_in(keys[9], 71), 0)
    y_operators = draw_y_operators(jax.random.fold_in(keys[9], 71), 0)
    viscosity = jnp.clip(jnp.exp(jax.random.uniform(keys[3], (FIELDS,), jnp.float32, math.log(0.1), math.log(1.0))), 0.1, 1.0)
    wall_tile = with_ends(jax.random.randint(keys[4], (DEVICES * WALL_DEV,), 0, NZ * (NX // N_PX)), jax.random.fold_in(keys[4], 1), 0, (NZ * (NX // N_PX)) - 1).astype(jnp.int32)
    wall_owner_keys = jax.random.split(jax.random.fold_in(keys[5], 1), (DEVICES * WALL_DEV) // WALL_DEV)
    wall_owner_turns = jax.random.permutation(jax.random.fold_in(keys[5], 3), (DEVICES * WALL_DEV) // WALL_DEV)
    wall_owner = jax.vmap(lambda own, number: assign_block(jax.random.fold_in(keys[5], 2), own, number, WALL_DEV, DEVICES, 1, CAP, 2))(wall_owner_keys, wall_owner_turns).reshape((DEVICES * WALL_DEV, 1))
    wall_row = with_ends(jax.random.randint(keys[6], (DEVICES * WALL_DEV,), 0, SR), jax.random.fold_in(keys[6], 1), 0, SR - 1).astype(jnp.int32)
    solid_temp = gaussian(keys[7], (SOLID_ROWS, NY), 1.0, 6.0, ((0, 8), (1, 4)), jnp.float32)
    conductivity = jnp.clip(jnp.exp(math.log(1.0) - 1.609438 * jax.random.uniform(keys[8], (SOLID_ROWS, NY), jnp.float32) ** steps_of(keys[8], (SOLID_ROWS, NY), ((0, 8), (1, 4)), -0.2, 0.2)), 0.2, 1.0)
    return dict(fields=fields, x_operators=x_operators, y_operators=y_operators, viscosity=viscosity, wall_tile=wall_tile, wall_owner=wall_owner, wall_row=wall_row, solid_temp=solid_temp, conductivity=conductivity)


time_step = 0.25
wall_gain = 0.5
diffusion_rate = 0.24
source_gain = 0.1


def pass_x(fields, operators, viscosity):
    mats = operators.astype(jnp.float32)
    speed = fields[0].astype(jnp.float32)

    def single(pair):
        field, rate = pair
        values = field.astype(jnp.float32)
        result = jnp.einsum('oij,zjy->oziy', mats, values, precision=lax.Precision.HIGHEST)
        return (result[2] + time_step * (-speed * result[0] + rate * result[1])).astype(jnp.bfloat16)

    return lax.map(single, (fields, viscosity))


def pass_y(fields, operators, viscosity):
    mats = operators.astype(jnp.float32)
    speed = fields[1].astype(jnp.float32)

    def single(pair):
        field, rate = pair
        values = field.astype(jnp.float32)
        result = jnp.einsum('oij,zxj->ozxi', mats, values, precision=lax.Precision.HIGHEST)
        return (result[2] + time_step * (-speed * result[0] + rate * result[1])).astype(jnp.bfloat16)

    return lax.map(single, (fields, viscosity))


def reference(fields, x_operators, y_operators, viscosity, wall_tile, wall_owner, wall_row, solid_temp, conductivity):
    half_step = pass_x(fields, x_operators, viscosity)
    new_fields = pass_y(half_step, y_operators, viscosity)
    cells_x = NX // N_PX
    cells_y = NY // N_PY
    sender = jnp.arange(DEVICES * WALL_DEV, dtype=jnp.int32) // WALL_DEV
    send_px = sender // N_PY
    send_py = sender % N_PY
    layer = wall_tile // cells_x
    column_x = send_px * cells_x + wall_tile % cells_x
    offsets = jnp.arange(cells_y, dtype=jnp.int32)
    theta = new_fields[3]
    values = theta[layer[:, None], column_x[:, None], send_py[:, None] * cells_y + offsets[None, :]]
    flux = wall_gain * values.astype(jnp.float32)
    owner = wall_owner[:, 0]
    target_row = (owner // N_PY) * SR + wall_row
    target_col = (owner % N_PY) * cells_y
    source = jnp.zeros(solid_temp.shape, jnp.float32)
    source = source.at[target_row[:, None], target_col[:, None] + offsets[None, :]].add(flux)
    temp = solid_temp
    kpad = jnp.pad(conductivity, 1)
    for _ in range(COND_STEPS):
        tpad = jnp.pad(temp, 1)
        near = [(tpad[2:, 1:-1], kpad[2:, 1:-1]), (tpad[:-2, 1:-1], kpad[:-2, 1:-1]),
                (tpad[1:-1, 2:], kpad[1:-1, 2:]), (tpad[1:-1, :-2], kpad[1:-1, :-2])]
        laplace = jnp.zeros(temp.shape, jnp.float32)
        for tnear, knear in near:
            laplace = laplace + 0.5 * (conductivity + knear) * (tnear - temp)
        temp = temp + diffusion_rate * laplace + source_gain * source
    return new_fields, temp
```

```python
import functools

import jax
import jax.numpy as jnp
from jax import lax
from jax.experimental import pallas as pl
from jax.experimental.pallas import tpu as pltpu
from jax.sharding import PartitionSpec as P

COND_STEPS = 8

time_step = 0.25
wall_gain = 0.5
diffusion_rate = 0.24
source_gain = 0.1

U, V, W, THETA = 0, 1, 2, 3
FORWARD = (U, V, THETA, W)
BACK = (V, THETA, U, W)
VMEM_BYTES = 40 * 1024 * 1024

smem = pl.BlockSpec(memory_space=pltpu.SMEM)
vmem = pl.BlockSpec(memory_space=pltpu.VMEM)
anywhere = pl.BlockSpec(memory_space=pl.ANY)


def params():
    return pltpu.CompilerParams(vmem_limit_bytes=VMEM_BYTES)


def with_halo(block, sides, width):
    for axis, dim in sides:
        count = lax.axis_size(axis)
        forward = [(i, i + 1) for i in range(count - 1)]
        backward = [(target, source) for source, target in forward]
        low = lax.ppermute(
            lax.slice_in_dim(block, block.shape[dim] - width, None, axis=dim), axis, forward
        )
        high = lax.ppermute(lax.slice_in_dim(block, 0, width, axis=dim), axis, backward)
        block = jnp.concatenate([low, block, high], axis=dim)
    return block


def shuffle(inputs, place, take):
    outer, block = len(inputs), inputs[0].shape[1:]
    inner = inputs[0].shape[0]

    def kernel(at, *refs):
        for k in range(inner):
            for j in range(outer):
                refs[outer + k][at[0] ^ j] = refs[j][at[1] ^ k]

    return pl.pallas_call(
        kernel,
        in_specs=[smem] + [vmem] * outer,
        out_specs=[vmem] * inner,
        out_shape=[jax.ShapeDtypeStruct((outer,) + block, inputs[0].dtype)] * inner,
        compiler_params=params(),
        name="shuffle",
    )(jnp.stack([place, take]), *inputs)


def x_pass(field, at, operators, viscosity, own, others, speed):
    groups, members = len(own), len(others) + 1
    blocks, xb, yb = own[0].shape
    part = blocks // members
    width = part * yb
    length = groups * members * xb
    many = min(groups, max(1, 256 // xb))
    steps = groups // many
    first = field == U

    def kernel(at_ref, visc_ref, op_ref, *refs):
        own_refs, other_refs = refs[:groups], refs[groups : groups + members - 1]
        rest = refs[groups + members - 1 :]
        if first:
            outs, lines = rest[:members], rest[members]
        else:
            speed_ref, outs, lines = rest[0], rest[1 : 1 + members], rest[1 + members]
        step = pl.program_id(0)
        q, m = at_ref[0], at_ref[1]

        def start(group, member):
            return pl.multiple_of(((q ^ group) * members + (m ^ member)) * xb, xb)

        @pl.when(step == 0)
        def _():
            for t in range(groups):
                for j in range(part):
                    lines[pl.ds(start(t, 0), xb), j * yb : (j + 1) * yb] = own_refs[t][j]
                    for r in range(1, members):
                        lines[pl.ds(start(t, r), xb), j * yb : (j + 1) * yb] = other_refs[r - 1][t, j]

        result = jnp.dot(
            op_ref[...].reshape(3 * many * xb, length), lines[...], preferred_element_type=jnp.float32
        ).reshape(3, many, xb, width)
        turn = step // steps
        for c in range(many):
            if first:
                row = ((step % steps * many + c) * members + (m ^ turn)) * xb
                u = lines[pl.ds(pl.multiple_of(row, xb), xb), :]
            else:
                u = speed_ref[c, 0]
            value = result[2, c] + time_step * (
                -u.astype(jnp.float32) * result[0, c] + visc_ref[field] * result[1, c]
            )
            value = value.astype(jnp.bfloat16)
            for r in range(members):

                @pl.when(turn == r)
                def _():
                    outs[r][c] = value

    def out_block(r):
        return pl.BlockSpec(
            (many, xb, width), lambda i, at: (jnp.clip(i - r * steps, 0, steps - 1), 0, 0)
        )

    def rows(i, at):
        return i % steps, at[1] ^ (i // steps), 0, 0

    in_specs = [
        smem,
        pl.BlockSpec((3, many, 1, xb, length), lambda i, at: (0,) + rows(i, at)),
    ]
    in_specs += [pl.BlockSpec((part, xb, yb), lambda i, at: (at[1], 0, 0))] * groups
    in_specs += [pl.BlockSpec((groups, part, xb, yb), lambda i, at: (0, 0, 0, 0))] * (members - 1)
    args = [viscosity, operators.reshape(3, groups, members, xb, length), *own, *others]
    out_specs = [out_block(r) for r in range(members)]
    out_shape = [jax.ShapeDtypeStruct((groups, xb, width), jnp.bfloat16)] * members
    scratch = []
    if first:
        out_specs.append(pl.BlockSpec((length, width), lambda i, at: (0, 0)))
        out_shape.append(jax.ShapeDtypeStruct((length, width), jnp.bfloat16))
    else:
        in_specs.append(pl.BlockSpec((many, 1, xb, width), rows))
        args.append(speed.reshape(groups, members, xb, width))
        scratch = [pltpu.VMEM((length, width), jnp.bfloat16)]
    outs = pl.pallas_call(
        kernel,
        grid_spec=pltpu.PrefetchScalarGridSpec(
            num_scalar_prefetch=1,
            grid=(steps * members,),
            in_specs=in_specs,
            out_specs=out_specs,
            scratch_shapes=scratch,
        ),
        out_shape=out_shape,
        compiler_params=params(),
        cost_estimate=pl.CostEstimate(
            flops=6 * length * length * width,
            bytes_accessed=6 * length * length + 4 * length * width,
            transcendentals=0,
        ),
        name="x_pass",
    )(at, *args)
    return outs[:members], outs[members] if first else speed


def y_pass(field, at, operators, viscosity, own, others, speed, yb):
    groups, xb, width = own.shape
    members = len(others) + 1
    length = width * members
    blocks = length // yb
    first = field == V

    def kernel(at_ref, visc_ref, op_ref, *refs):
        sources, rest = refs[:members], refs[members:]
        if first:
            outs, lines = rest[:groups], rest[groups]
        else:
            speed_ref, outs, lines = rest[0], rest[1 : 1 + groups], rest[1 + groups]
        step = pl.program_id(0)
        q, m = at_ref[0], at_ref[1]

        @pl.when(step == 0)
        def _():
            for t in range(groups):
                for r in range(members):
                    columns = pl.ds(pl.multiple_of((m ^ r) * width, width), width)
                    lines[t * xb : (t + 1) * xb, columns] = sources[r][q ^ t]

        result = lax.dot_general(
            lines[...],
            op_ref[...].reshape(3 * yb, length),
            (((1,), (1,)), ((), ())),
            preferred_element_type=jnp.float32,
        )
        if first:
            v = lines[:, pl.ds(pl.multiple_of(step * yb, yb), yb)]
        else:
            v = speed_ref[...]
        value = result[:, 2 * yb :] + time_step * (
            -v.astype(jnp.float32) * result[:, :yb] + visc_ref[field] * result[:, yb : 2 * yb]
        )
        value = value.astype(jnp.bfloat16)
        for t in range(groups):
            outs[t][0] = value[t * xb : (t + 1) * xb]

    in_specs = [smem, pl.BlockSpec((3, yb, length), lambda i, at: (0, i, 0))]
    in_specs += [pl.BlockSpec((groups, xb, width), lambda i, at: (0, 0, 0))] * members
    args = [viscosity, operators, own, *others]
    out_specs = [pl.BlockSpec((1, xb, yb), lambda i, at: (i, 0, 0))] * groups
    out_shape = [jax.ShapeDtypeStruct((blocks, xb, yb), jnp.bfloat16)] * groups
    scratch = []
    if first:
        out_specs.append(pl.BlockSpec((groups * xb, length), lambda i, at: (0, 0)))
        out_shape.append(jax.ShapeDtypeStruct((groups * xb, length), jnp.bfloat16))
    else:
        in_specs.append(pl.BlockSpec((groups * xb, yb), lambda i, at: (0, i)))
        args.append(speed)
        scratch = [pltpu.VMEM((groups * xb, length), jnp.bfloat16)]
    outs = pl.pallas_call(
        kernel,
        grid_spec=pltpu.PrefetchScalarGridSpec(
            num_scalar_prefetch=1,
            grid=(blocks,),
            in_specs=in_specs,
            out_specs=out_specs,
            scratch_shapes=scratch,
        ),
        out_shape=out_shape,
        compiler_params=params(),
        cost_estimate=pl.CostEstimate(
            flops=6 * length * length * groups * xb,
            bytes_accessed=6 * length * length + 4 * length * groups * xb,
            transcendentals=0,
        ),
        name="y_pass",
    )(at, *args)
    return outs[:groups], outs[groups] if first else speed


def put(buffer, pieces, field, b, shape):
    count, groups = len(pieces), pieces[0].shape[0]

    def kernel(at, *refs):
        out, sems = refs[-2], refs[-1]
        copies = [
            pltpu.make_async_copy(
                refs[s], out.at[field, pl.ds((at[0] ^ s) * groups, groups)], sems.at[s]
            )
            for s in range(count)
        ]
        for copy in copies:
            copy.start()
        for copy in copies:
            copy.wait()

    extra = [] if buffer is None else [buffer]
    return pl.pallas_call(
        kernel,
        in_specs=[smem] + [anywhere] * (count + len(extra)),
        out_specs=anywhere,
        out_shape=jax.ShapeDtypeStruct(shape, pieces[0].dtype),
        scratch_shapes=[pltpu.SemaphoreType.DMA((count,))],
        input_output_aliases={} if buffer is None else {1 + count: 0},
        compiler_params=params(),
        name="put",
    )(b.reshape(1), *pieces, *extra)


def wall_lines(pieces, b, tile, slot, slots):
    groups, xb, yb = pieces[0].shape
    span = groups * xb
    count = tile.shape[0]

    def kernel(at, tile_ref, slot_ref, *refs):
        places = lax.broadcasted_iota(jnp.int32, (count, span), 1)
        lines = jnp.zeros((count, yb), jnp.float32)
        for s, piece in enumerate(refs[:-1]):
            chosen = tile_ref[...] == places + (at[0] ^ s) * span
            lines = lines + jnp.dot(
                chosen.astype(jnp.float32).astype(jnp.bfloat16),
                piece[...].reshape(span, yb),
                preferred_element_type=jnp.float32,
            )
        filled = slot_ref[...] == lax.broadcasted_iota(jnp.int32, (slots, count), 0)
        refs[-1][...] = jnp.dot(
            filled.astype(jnp.float32).astype(jnp.bfloat16),
            lines.astype(jnp.bfloat16),
            preferred_element_type=jnp.float32,
        ).astype(jnp.bfloat16)

    return pl.pallas_call(
        kernel,
        in_specs=[smem] + [vmem] * (2 + len(pieces)),
        out_specs=vmem,
        out_shape=jax.ShapeDtypeStruct((slots, yb), jnp.bfloat16),
        compiler_params=params(),
        name="wall_lines",
    )(b.reshape(1), tile.reshape(-1, 1), slot.reshape(1, -1), *pieces)


def conduct(temp, faces, heat, rows, columns, margin):
    def kernel(temp_ref, faces_ref, heat_ref, out_ref):
        t = temp_ref[...]
        high, wide = t.shape
        for _ in range(COND_STEPS):
            change = heat_ref[...]
            for n, (shift, dim) in enumerate(((high - 1, 0), (1, 0), (wide - 1, 1), (1, 1))):
                change = change + faces_ref[n] * (pltpu.roll(t, shift, dim) - t)
            t = t + change
        out_ref[...] = t[margin : margin + rows, margin : margin + columns]

    return pl.pallas_call(
        kernel,
        in_specs=[vmem] * 3,
        out_specs=vmem,
        out_shape=jax.ShapeDtypeStruct((rows, columns), jnp.float32),
        compiler_params=params(),
        name="conduct",
    )(temp, faces, heat)


def on_device(
    fields,
    x_operators,
    y_operators,
    viscosity,
    wall_tile,
    wall_owner,
    wall_row,
    solid_temp,
    conductivity,
):
    across_px, across_py = lax.axis_size("px"), lax.axis_size("py")
    devices = across_px * across_py
    layers, xb, yb = fields.shape[1:]
    members = devices // layers
    groups = across_px // members
    a, b = lax.axis_index("px"), lax.axis_index("py")
    q, m = a // members, a % members
    at = jnp.stack([q, m])

    def along_py(piece, s):
        return lax.ppermute(piece, "py", [(i, i ^ s) for i in range(across_py)])

    def along_groups(piece, t):
        return lax.ppermute(piece, "px", [(i, i ^ (t * members)) for i in range(across_px)])

    def along_members(piece, r):
        return lax.ppermute(piece, "px", [(i, i ^ r) for i in range(across_px)])

    margin = COND_STEPS
    sides = (("px", 0), ("py", 1))
    solid = with_halo(
        jnp.stack([solid_temp, conductivity]), (("px", 1), ("py", 2)), margin
    )
    rows, columns = solid_temp.shape
    high, wide = solid.shape[1:]
    lanes = -(-wide // 128) * 128
    solid = jnp.pad(solid, ((0, 0), (0, 0), (0, lanes - wide)))
    row_index = a * rows - margin + jnp.arange(high, dtype=jnp.int32)
    col_index = b * columns - margin + jnp.arange(lanes, dtype=jnp.int32)
    inside = ((row_index >= 0) & (row_index < across_px * rows))[:, None] & (
        (col_index >= 0) & (col_index < across_py * columns)
    )[None, :]
    kappa = solid[1]
    faces = jnp.stack(
        [
            jnp.where(inside, diffusion_rate * 0.5 * (kappa + jnp.roll(kappa, shift, dim)), 0.0)
            for shift, dim in ((-1, 0), (1, 0), (-1, 1), (1, 1))
        ]
    )

    count = wall_tile.shape[0]
    owner = wall_owner[:, 0]
    capacity = max(2, 4 * count // devices)
    slots = devices * capacity
    order = jnp.arange(count, dtype=jnp.int32)
    earlier = (owner[:, None] == owner[None, :]) & (order[None, :] < order[:, None])
    slot = owner * capacity + jnp.sum(earlier.astype(jnp.int32), axis=1)
    filled = slot[None, :] == jnp.arange(slots, dtype=jnp.int32)[:, None]
    labels = jnp.sum(jnp.where(filled, wall_row[None, :] + 1, 0), axis=1) - 1
    tags = lax.all_to_all(
        labels.reshape(devices, capacity), ("px", "py"), split_axis=0, concat_axis=0, tiled=True
    )

    part = across_py // members
    kept, speed = {}, None
    for f in FORWARD:
        pieces = [
            lax.dynamic_slice_in_dim(fields[f], (b ^ s) * groups, groups, axis=0)
            for s in range(across_py)
        ]
        pieces = [pieces[0]] + [along_py(pieces[s], s) for s in range(1, across_py)]
        sending = shuffle(pieces, b, q)
        own = [sending[0]] + [along_groups(sending[t], t) for t in range(1, groups)]
        others = [
            along_members(
                jnp.stack(
                    [lax.dynamic_slice_in_dim(o, (m ^ r) * part, part, axis=0) for o in own]
                ),
                r,
            )
            for r in range(1, members)
        ]
        half, speed = x_pass(f, at, x_operators, viscosity, own, others, speed)
        kept[f] = (half[0], [along_members(half[r], r) for r in range(1, members)])

    new_fields, speed = None, None
    for f in BACK:
        own, others = kept[f]
        sending, speed = y_pass(f, at, y_operators, viscosity, own, others, speed, yb)
        own = [sending[0]] + [along_groups(sending[t], t) for t in range(1, groups)]
        sending = shuffle(own, q, b)
        pieces = [sending[0]] + [along_py(sending[s], s) for s in range(1, across_py)]
        new_fields = put(new_fields, pieces, f, b, fields.shape)
        if f == THETA:
            flux = wall_lines(pieces, b, wall_tile, slot, slots)
            arrived = lax.all_to_all(
                flux.reshape(devices, capacity, yb),
                ("px", "py"),
                split_axis=0,
                concat_axis=0,
                tiled=True,
            ).reshape(slots, yb)
            selector = tags.reshape(-1)[None, :] == jnp.arange(rows, dtype=jnp.int32)[:, None]
            source = (wall_gain * source_gain) * jnp.dot(
                selector.astype(jnp.bfloat16), arrived, preferred_element_type=jnp.float32
            )
            heat = with_halo(source, sides, margin)
            heat = jnp.pad(heat, ((0, 0), (0, lanes - wide)))
            new_solid = conduct(solid[0], faces, heat, rows, columns, margin)
    return new_fields, new_solid


def solution(mesh):
    return jax.shard_map(
        on_device,
        mesh=mesh,
        in_specs=(
            P(None, None, "px", "py"),
            P(),
            P(),
            P(),
            P(("px", "py")),
            P(("px", "py"), None),
            P(("px", "py")),
            P("px", "py"),
            P("px", "py"),
        ),
        out_specs=(P(None, None, "px", "py"), P("px", "py")),
        check_vma=False,
    )
```

```python
import jax
import jax.numpy as jnp
from jax import lax
from jax.experimental import pallas as pl
from jax.experimental.pallas import tpu as pltpu
from jax.sharding import PartitionSpec as P

COND_STEPS = 8

time_step = 0.25
wall_gain = 0.5
diffusion_rate = 0.24
source_gain = 0.1

U, V, W, THETA = 0, 1, 2, 3
VMEM_BYTES = 20 * 1024 * 1024

smem = pl.BlockSpec(memory_space=pltpu.SMEM)
anywhere = pl.BlockSpec(memory_space=pl.ANY)


def with_halo(block, sides, width):
    for axis, dim in sides:
        count = lax.axis_size(axis)
        forward = [(i, i + 1) for i in range(count - 1)]
        backward = [(target, source) for source, target in forward]
        low = lax.ppermute(
            lax.slice_in_dim(block, block.shape[dim] - width, None, axis=dim), axis, forward
        )
        high = lax.ppermute(lax.slice_in_dim(block, 0, width, axis=dim), axis, backward)
        block = jnp.concatenate([low, block, high], axis=dim)
    return block


def in_order(part):
    return part % 128 == 0


class Chain:
    def __init__(self, at):
        self.at = at
        self.last = []

    def run(
        self, name, kernel, args, in_specs, out_specs, out_shape, grid=(1,), scratch=(), aliases=None, flops=0
    ):
        count = len(args)
        tokens = [x for x in self.last if not any(x is y for y in args)]

        def body(at_ref, *refs):
            kernel(at_ref, *refs[:count], *refs[count + len(tokens) :])

        moved = sum(x.size * x.dtype.itemsize for x in out_shape)
        outs = pl.pallas_call(
            body,
            grid_spec=pltpu.PrefetchScalarGridSpec(
                num_scalar_prefetch=1,
                grid=grid,
                in_specs=list(in_specs) + [anywhere] * len(tokens),
                out_specs=out_specs,
                scratch_shapes=list(scratch),
            ),
            out_shape=out_shape,
            input_output_aliases=aliases or {},
            compiler_params=pltpu.CompilerParams(vmem_limit_bytes=VMEM_BYTES),
            cost_estimate=pl.CostEstimate(flops=flops, bytes_accessed=2 * moved, transcendentals=0),
            name=name,
        )(self.at, *args, *tokens)
        self.last = [outs[0]]
        return outs


def whole(shape):
    return pl.BlockSpec(shape, lambda i, at: (0,) * len(shape))


def like(pieces):
    return [whole(piece.shape) for piece in pieces]


def cut(chain, fields, which, across_px, across_py):
    layers, xb, yb = fields.shape[1:]
    groups = layers // across_py
    members = across_px // groups
    part = yb // members

    def kernel(at, *refs):
        for n in range(len(which)):
            for g in range(groups):
                for k in range(members):
                    refs[-1][g * members + k, 0, n] = refs[n][0, g, :, k * part : (k + 1) * part]

    def field(f):
        return pl.BlockSpec((1, groups, xb, yb), lambda i, at: (f, i, 0, 0))

    shape = (across_px, across_py, len(which), xb, part)
    return chain.run(
        "cut",
        kernel,
        [fields] * len(which),
        [field(f) for f in which],
        [pl.BlockSpec((across_px, 1) + shape[2:], lambda i, at: (0, i, 0, 0, 0))],
        [jax.ShapeDtypeStruct(shape, fields.dtype)],
        grid=(across_py,),
    )[0]


def x_pass(chain, field, operators, viscosity, arrived, n, members, speed):
    across_px, across_py, _, xb, part = arrived.shape
    width = across_py * part
    length = across_px * xb
    rows = xb // members
    many = min(across_px, max(1, 256 // rows))
    steps = across_px // many
    first = field == U

    def kernel(at, visc_ref, op_ref, arrived_ref, *refs):
        if first:
            outs, lines = refs[:-1], refs[-1]
        else:
            speed_ref, outs, lines = refs[0], refs[1:-1], refs[-1]
        step = pl.program_id(0)
        turn, place = step // steps, step % steps

        @pl.when(step == 0)
        def _():
            for x in range(across_px):
                for y in range(across_py):
                    lines[x * xb : (x + 1) * xb, y * part : (y + 1) * part] = arrived_ref[x, y, 0]

        result = jnp.dot(
            op_ref[...].reshape(3 * many * rows, length), lines[...], preferred_element_type=jnp.float32
        ).reshape(3, many, rows, width)
        for c in range(many):
            if first:
                row = (place * many + c) * xb + (at[1] ^ turn) * rows
                u = lines[pl.ds(pl.multiple_of(row, rows), rows), :]
            else:
                u = speed_ref[c, 0]
            value = result[2, c] + time_step * (
                -u.astype(jnp.float32) * result[0, c] + visc_ref[field] * result[1, c]
            )
            value = value.astype(jnp.bfloat16)
            for r in range(members):

                @pl.when(turn == r)
                def _():
                    outs[r][c] = value

    def out_block(r):
        return pl.BlockSpec(
            (many, rows, width), lambda i, at: (jnp.clip(i - r * steps, 0, steps - 1), 0, 0)
        )

    def place_of(i, at):
        return i % steps, at[1] ^ (i // steps), 0, 0

    in_specs = [
        smem,
        pl.BlockSpec((3, many, 1, rows, length), lambda i, at: (0,) + place_of(i, at)),
        pl.BlockSpec((across_px, across_py, 1, xb, part), lambda i, at: (0, 0, n, 0, 0)),
    ]
    args = [viscosity, operators.reshape(3, across_px, members, rows, length), arrived]
    out_specs = [out_block(r) for r in range(members)]
    out_shape = [jax.ShapeDtypeStruct((across_px, rows, width), jnp.bfloat16)] * members
    scratch = []
    if first:
        out_specs.append(whole((length, width)))
        out_shape.append(jax.ShapeDtypeStruct((length, width), jnp.bfloat16))
    else:
        in_specs.append(pl.BlockSpec((many, 1, rows, width), place_of))
        args.append(speed.reshape(across_px, members, rows, width))
        scratch = [pltpu.VMEM((length, width), jnp.bfloat16)]
    outs = chain.run(
        "x_pass",
        kernel,
        args,
        in_specs,
        out_specs,
        out_shape,
        grid=(steps * members,),
        scratch=scratch,
        flops=6 * length * length * width,
    )
    return outs[:members], outs[members] if first else speed


def y_pass(chain, field, operators, viscosity, parts, speed, buffer, n, shape):
    across_px, rows, width = parts[0].shape
    members = len(parts)
    yb = shape[-1]
    part = yb // members
    length = width * members
    blocks = length // yb
    first = field == V
    extra = [] if buffer is None else [buffer]

    def kernel(at, visc_ref, op_ref, *refs):
        part_refs, rest = refs[:members], refs[members:]
        if first:
            out, speed_ref, lines = rest[-3:]
        else:
            speed_ref, out, lines = rest[0], rest[-2], rest[-1]
        step = pl.program_id(0)

        @pl.when(step == 0)
        def _():
            for r in range(members):
                values = part_refs[r][...].reshape(across_px * rows, width)
                if in_order(part):
                    for y in range(blocks):
                        start = pl.multiple_of(y * yb + (at[1] ^ r) * part, part)
                        lines[:, pl.ds(start, part)] = values[:, y * part : (y + 1) * part]
                else:
                    lines[:, pl.ds(pl.multiple_of((at[1] ^ r) * width, width), width)] = values
            if first:
                for y in range(blocks):
                    if in_order(part):
                        speed_ref[y] = lines[:, y * yb : (y + 1) * yb]
                    else:
                        for k in range(members):
                            start = k * width + y * part
                            speed_ref[y, :, k * part : (k + 1) * part] = lines[:, start : start + part]

        result = lax.dot_general(
            lines[...],
            op_ref[...].reshape(3 * yb, length),
            (((1,), (1,)), ((), ())),
            preferred_element_type=jnp.float32,
        )
        v = speed_ref[step if first else 0]
        value = result[:, 2 * yb :] + time_step * (
            -v.astype(jnp.float32) * result[:, :yb] + visc_ref[field] * result[:, yb : 2 * yb]
        )
        out[:, 0, 0] = value.astype(jnp.bfloat16).reshape(across_px, rows, yb)

    in_specs = [smem, pl.BlockSpec((3, yb, length), lambda i, at: (0, i, 0))] + like(parts)
    args = [viscosity, operators, *parts]
    out_specs = [pl.BlockSpec((across_px, 1, 1, rows, yb), lambda i, at: (0, i, n, 0, 0))]
    out_shape = [jax.ShapeDtypeStruct(shape, jnp.bfloat16)]
    if first:
        out_specs.append(whole((blocks, across_px * rows, yb)))
        out_shape.append(jax.ShapeDtypeStruct((blocks, across_px * rows, yb), jnp.bfloat16))
    else:
        in_specs.append(pl.BlockSpec((1, across_px * rows, yb), lambda i, at: (i, 0, 0)))
        args.append(speed)
    outs = chain.run(
        "y_pass",
        kernel,
        args + extra,
        in_specs + [anywhere] * len(extra),
        out_specs,
        out_shape,
        grid=(blocks,),
        scratch=[pltpu.VMEM((across_px * rows, length), jnp.bfloat16)],
        aliases={1 + len(args): 0} if extra else {},
        flops=6 * length * length * across_px * rows,
    )
    return outs[0], outs[1] if first else speed


def put(chain, buffer, arrived, which, shape):
    across_px, across_py, many, rows, yb = arrived.shape
    layers, xb = shape[1:3]
    groups = layers // across_py
    members = across_px // groups

    def kernel(at, arrived_ref, *refs):
        for g in range(groups):
            for k in range(members):
                refs[-1][0, g, k * rows : (k + 1) * rows] = arrived_ref[g * members + k, 0, 0]

    extra = [] if buffer is None else [buffer]
    first, stride = which[0], which[-1] - which[0]
    return chain.run(
        "put",
        kernel,
        [arrived, *extra],
        [pl.BlockSpec((across_px, 1, 1, rows, yb), lambda n, i, at: (0, i, n, 0, 0))]
        + [anywhere] * len(extra),
        [pl.BlockSpec((1, groups, xb, yb), lambda n, i, at: (first + n * stride, i, 0, 0))],
        [jax.ShapeDtypeStruct(shape, arrived.dtype)],
        grid=(many, across_py),
        aliases={2: 0} if extra else {},
    )[0]


def wall_lines(chain, arrived, n, line, slot, capacity):
    across_px, across_py, _, rows, yb = arrived.shape
    count, span = line.shape[0], across_px * across_py * rows
    slots = across_px * across_py * capacity

    def kernel(at, line_ref, slot_ref, arrived_ref, *refs):
        chosen = line_ref[...] == lax.broadcasted_iota(jnp.int32, (count, span), 1)
        flux = jnp.dot(
            chosen.astype(jnp.float32).astype(jnp.bfloat16),
            arrived_ref[...].reshape(span, yb),
            preferred_element_type=jnp.float32,
        )
        filled = slot_ref[...] == lax.broadcasted_iota(jnp.int32, (slots, count), 0)
        refs[-1][...] = jnp.dot(
            filled.astype(jnp.float32).astype(jnp.bfloat16),
            flux.astype(jnp.bfloat16),
            preferred_element_type=jnp.float32,
        ).reshape(across_px, across_py, capacity, yb)
        for s in range(across_px):
            refs[s][...] = refs[-1][at[7] ^ s].astype(jnp.bfloat16)

    args = [line.reshape(-1, 1), slot.reshape(1, -1)]
    shape = (across_py, capacity, yb)
    return chain.run(
        "wall_lines",
        kernel,
        args + [arrived],
        like(args)
        + [pl.BlockSpec((across_px, across_py, 1, rows, yb), lambda i, at: (0, 0, n, 0, 0))],
        [whole(shape)] * across_px,
        [jax.ShapeDtypeStruct(shape, jnp.bfloat16)] * across_px,
        scratch=[pltpu.VMEM((across_px,) + shape, jnp.float32)],
    )


def wall_columns(chain, pieces):
    across_px, (across_py, capacity, yb) = len(pieces), pieces[0].shape

    def kernel(at, *refs):
        for s in range(across_py):
            for t in range(across_px):
                refs[across_px + s][at[7] ^ t] = refs[t][at[2] ^ s]

    shape = (across_px, capacity, yb)
    return chain.run(
        "wall_columns",
        kernel,
        pieces,
        like(pieces),
        [whole(shape)] * across_py,
        [jax.ShapeDtypeStruct(shape, jnp.bfloat16)] * across_py,
    )


def add_flux(chain, tags, arrived, solid_temp, conductivity):
    rows, columns = solid_temp.shape
    across_py, (across_px, capacity, _) = len(arrived), arrived[0].shape

    def kernel(at, temp_ref, kappa_ref, *refs):
        tag_refs, flux_refs, out = refs[:across_py], refs[across_py:-1], refs[-1]
        out[0] = temp_ref[...]
        out[1] = kappa_ref[...]
        places = lax.broadcasted_iota(jnp.int32, (rows, capacity), 0)
        source = jnp.zeros((rows, columns), jnp.float32)
        for s in range(across_py):
            chosen = [tag_refs[s][at[7] ^ t] == places for t in range(across_px)]
            chosen = jnp.concatenate([c.astype(jnp.float32) for c in chosen], axis=1)
            source = source + jnp.dot(
                chosen.astype(jnp.bfloat16),
                flux_refs[s][...].reshape(across_px * capacity, columns),
                preferred_element_type=jnp.float32,
            )
        out[2] = (wall_gain * source_gain) * source

    args = [solid_temp, conductivity, *tags, *arrived]
    return chain.run(
        "add_flux",
        kernel,
        args,
        like(args),
        [whole((3, rows, columns))],
        [jax.ShapeDtypeStruct((3, rows, columns), jnp.float32)],
    )[0]


def conduct(chain, solid, rows, columns, margin):
    high, wide = solid.shape[1:]

    def kernel(at, solid_ref, out):
        t, kappa, heat = solid_ref[0], solid_ref[1], solid_ref[2]
        row = lax.broadcasted_iota(jnp.int32, (high, wide), 0) + at[3]
        col = lax.broadcasted_iota(jnp.int32, (high, wide), 1) + at[4]
        inside = (row >= 0) & (row < at[5]) & (col >= 0) & (col < at[6])
        moves = ((high - 1, 0), (1, 0), (wide - 1, 1), (1, 1))
        faces = [
            jnp.where(inside, diffusion_rate * 0.5 * (kappa + pltpu.roll(kappa, shift, dim)), 0.0)
            for shift, dim in moves
        ]
        for _ in range(COND_STEPS):
            change = heat
            for face, (shift, dim) in zip(faces, moves):
                change = change + face * (pltpu.roll(t, shift, dim) - t)
            t = t + change
        out[...] = t[margin : margin + rows, margin : margin + columns]

    return chain.run(
        "conduct",
        kernel,
        [solid],
        like([solid]),
        [whole((rows, columns))],
        [jax.ShapeDtypeStruct((rows, columns), jnp.float32)],
    )[0]


def on_device(
    fields,
    x_operators,
    y_operators,
    viscosity,
    wall_tile,
    wall_owner,
    wall_row,
    solid_temp,
    conductivity,
):
    across_px, across_py = lax.axis_size("px"), lax.axis_size("py")
    devices = across_px * across_py
    layers, xb, yb = fields.shape[1:]
    groups = layers // across_py
    members = across_px // groups
    a, b = lax.axis_index("px"), lax.axis_index("py")
    q, m = a // members, a % members
    rows, columns = solid_temp.shape
    margin = COND_STEPS
    at = jnp.stack(
        [
            q,
            m,
            b,
            a * rows - margin,
            b * columns - margin,
            across_px * rows,
            across_py * columns,
            a,
        ]
    ).astype(jnp.int32)
    chain = Chain(at)

    def along(axis, pieces):
        return [pieces[0]] + [
            lax.ppermute(piece, axis, [(i, i ^ s) for i in range(lax.axis_size(axis))])
            for s, piece in enumerate(pieces[1:], 1)
        ]

    def exchange(blocks):
        moved = lax.all_to_all(
            blocks.reshape((devices,) + blocks.shape[2:]),
            ("px", "py"),
            split_axis=0,
            concat_axis=0,
            tiled=True,
        )
        return moved.reshape(blocks.shape)

    lines, half, speeds = {}, {}, {}

    def forward(*which):
        moved = exchange(cut(chain, fields, which, across_px, across_py))
        for n, f in enumerate(which):
            lines[f] = moved, n

    def X(f):
        out, speeds[U] = x_pass(
            chain, f, x_operators, viscosity, *lines[f], members, speeds.get(U)
        )
        half[f] = along("px", out)

    y_columns = y_operators
    if not in_order(yb // members):
        y_columns = y_columns.reshape(3, -1, across_py, members, yb // members)
        y_columns = y_columns.swapaxes(2, 3).reshape(y_operators.shape)

    def Y(f, buffer, n, many):
        shape = (across_px, across_py, many, xb // members, yb)
        buffer, speeds[V] = y_pass(
            chain, f, y_columns, viscosity, half[f], speeds.get(V), buffer, n, shape
        )
        return buffer

    forward(U, V, THETA)
    forward(W)

    count = wall_tile.shape[0]
    owner = wall_owner[:, 0]
    capacity = max(2, 4 * count // devices)
    slots = devices * capacity
    order = jnp.arange(count, dtype=jnp.int32)
    earlier = (owner[:, None] == owner[None, :]) & (order[None, :] < order[:, None])
    slot = owner * capacity + jnp.sum(earlier.astype(jnp.int32), axis=1)
    layer, x = wall_tile // xb, wall_tile % xb
    source = (layer % groups * members + x // (xb // members)) * across_py + layer // groups
    line = source * (xb // members) + x % (xb // members)
    filled = slot[None, :] == jnp.arange(slots, dtype=jnp.int32)[:, None]
    labels = jnp.sum(jnp.where(filled, wall_row[None, :] + 1, 0), axis=1) - 1
    labels = labels.reshape(across_px, across_py, capacity)
    tags = along(
        "px",
        [lax.dynamic_index_in_dim(labels, a ^ s, 0, keepdims=False) for s in range(across_px)],
    )
    tags = along(
        "py",
        [
            jnp.stack([lax.dynamic_index_in_dim(tag, b ^ s, 0) for tag in tags])
            for s in range(across_py)
        ],
    )

    chain.last += tags
    X(U), X(V)
    back = Y(V, None, 0, 2)
    X(THETA)
    back = exchange(Y(THETA, back, 1, 2))
    other = Y(U, None, 0, 2)
    X(W)
    other = exchange(Y(W, other, 1, 2))
    flux = along("px", wall_lines(chain, back, 1, line, slot, capacity))
    new_fields = put(chain, None, back, (V, THETA), fields.shape)
    flux = along("py", wall_columns(chain, flux))
    solid = add_flux(chain, tags, flux, solid_temp, conductivity)
    solid = with_halo(solid, (("px", 1), ("py", 2)), margin)
    solid = jnp.pad(solid, ((0, 0), (0, 0), (0, -solid.shape[2] % 128)))
    new_solid = conduct(chain, solid, rows, columns, margin)
    new_fields = put(chain, new_fields, other, (U, W), fields.shape)
    return new_fields, new_solid


def solution(mesh):
    return jax.shard_map(
        on_device,
        mesh=mesh,
        in_specs=(
            P(None, None, "px", "py"),
            P(),
            P(),
            P(),
            P(("px", "py")),
            P(("px", "py"), None),
            P(("px", "py")),
            P("px", "py"),
            P("px", "py"),
        ),
        out_specs=(P(None, None, "px", "py"), P("px", "py")),
        check_vma=False,
    )
```

```python
import jax
import jax.numpy as jnp
from jax import lax
from jax.experimental import pallas as pl
from jax.experimental.pallas import tpu as pltpu
from jax.sharding import PartitionSpec as P

COND_STEPS = 8

time_step = 0.25
wall_gain = 0.5
diffusion_rate = 0.24
source_gain = 0.1

U, V, W, THETA = 0, 1, 2, 3
SMALL_VMEM_BYTES = 16 * 1024 * 1024
MOST_VMEM_BYTES = 56 * 1024 * 1024

smem = pl.BlockSpec(memory_space=pltpu.SMEM)
anywhere = pl.BlockSpec(memory_space=pl.ANY)


def margins(block, axis, dim, width):
    count = lax.axis_size(axis)
    forward = [(i, i + 1) for i in range(count - 1)]
    backward = [(target, source) for source, target in forward]
    low = lax.ppermute(
        lax.slice_in_dim(block, block.shape[dim] - width, None, axis=dim), axis, forward
    )
    high = lax.ppermute(lax.slice_in_dim(block, 0, width, axis=dim), axis, backward)
    return low, high


def in_order(part):
    return part % 128 == 0


class Chain:
    def __init__(self, at):
        self.at = at
        self.last = []

    def run(
        self,
        name,
        kernel,
        args,
        in_specs,
        out_specs,
        out_shape,
        grid=(1,),
        scratch=(),
        aliases=None,
        flops=0,
        limit=MOST_VMEM_BYTES,
        free=False,
    ):
        count = len(args)
        tokens = [] if free else [x for x in self.last if not any(x is y for y in args)]

        def body(at_ref, *refs):
            kernel(at_ref, *refs[:count], *refs[count + len(tokens) :])

        moved = sum(x.size * x.dtype.itemsize for x in out_shape)
        outs = pl.pallas_call(
            body,
            grid_spec=pltpu.PrefetchScalarGridSpec(
                num_scalar_prefetch=1,
                grid=grid,
                in_specs=list(in_specs) + [anywhere] * len(tokens),
                out_specs=out_specs,
                scratch_shapes=list(scratch),
            ),
            out_shape=out_shape,
            input_output_aliases=aliases or {},
            compiler_params=pltpu.CompilerParams(vmem_limit_bytes=limit),
            cost_estimate=pl.CostEstimate(flops=flops, bytes_accessed=2 * moved, transcendentals=0),
            name=name,
        )(self.at, *args, *tokens)
        if not free:
            self.last = [min(outs, key=lambda x: x.size)]
        return outs


def whole(shape):
    return pl.BlockSpec(shape, lambda i, at: (0,) * len(shape))


def like(pieces):
    return [whole(piece.shape) for piece in pieces]


def cut(chain, fields, which, across_px, across_py):
    layers, xb, yb = fields.shape[1:]
    groups = layers // across_py
    members = across_px // groups
    part = yb // members

    def kernel(at, *refs):
        for n in range(len(which)):
            for g in range(groups):
                for k in range(members):
                    refs[-1][0, g * members + k, n] = refs[n][0, g, :, k * part : (k + 1) * part]

    def field(f):
        return pl.BlockSpec((1, groups, xb, yb), lambda i, at: (f, i, 0, 0))

    shape = (across_py, across_px, len(which), xb, part)
    return chain.run(
        "cut",
        kernel,
        [fields] * len(which),
        [field(f) for f in which],
        [pl.BlockSpec((1,) + shape[1:], lambda i, at: (i, 0, 0, 0, 0))],
        [jax.ShapeDtypeStruct(shape, fields.dtype)],
        grid=(across_py,),
        limit=MOST_VMEM_BYTES,
    )[0]


def x_pass(chain, which, operators, viscosity, arrived, members, speed):
    across_py, across_px, fields, xb, part = arrived.shape
    width = across_py * part
    length = across_px * xb
    rows = xb // members
    many = min(across_px, max(1, 256 // rows))
    steps = across_px // many
    first = which[0] == U

    def kernel(at, visc_ref, op_ref, arrived_ref, *refs):
        speed_ref, outs, lines = refs[0], refs[1:-1], refs[-1]
        if first:
            speed_ref, outs = refs[-2], refs[:-2]
        step = pl.program_id(0)
        turn, place = step // steps, step % steps

        @pl.when(step == 0)
        def _():
            for n in range(fields):
                for x in range(across_px):
                    for y in range(across_py):
                        start = n * width + y * part
                        lines[x * xb : (x + 1) * xb, start : start + part] = arrived_ref[y, x, n]
            if first:
                speed_ref[...] = lines[:, :width]

        block = op_ref[...].reshape(3 * many * rows, length)
        whole_result = jnp.dot(block, lines[...], preferred_element_type=jnp.float32)
        for n, field in enumerate(which):
            result = whole_result[:, n * width : (n + 1) * width].reshape(3, many, rows, width)
            for c in range(many):
                if first:
                    row = (place * many + c) * xb + (at[1] ^ turn) * rows
                    u = speed_ref[pl.ds(pl.multiple_of(row, rows), rows), :]
                else:
                    u = speed_ref[c, 0]
                value = result[2, c] + time_step * (
                    -u.astype(jnp.float32) * result[0, c] + visc_ref[field] * result[1, c]
                )
                value = value.astype(jnp.bfloat16)
                for r in range(members):

                    @pl.when(turn == r)
                    def _():
                        outs[n * members + r][c] = value

    def out_block(r):
        return pl.BlockSpec(
            (many, rows, width), lambda i, at: (jnp.clip(i - r * steps, 0, steps - 1), 0, 0)
        )

    def place_of(i, at):
        return i % steps, at[1] ^ (i // steps), 0, 0

    in_specs = [
        smem,
        pl.BlockSpec((3, many, 1, rows, length), lambda i, at: (0,) + place_of(i, at)),
        whole(arrived.shape),
    ]
    args = [viscosity, operators.reshape(3, across_px, members, rows, length), arrived]
    out_specs = [out_block(r) for _ in which for r in range(members)]
    out_shape = [jax.ShapeDtypeStruct((across_px, rows, width), jnp.bfloat16)] * len(out_specs)
    if first:
        out_specs.append(whole((length, width)))
        out_shape.append(jax.ShapeDtypeStruct((length, width), jnp.bfloat16))
    else:
        in_specs.append(pl.BlockSpec((many, 1, rows, width), place_of))
        args.append(speed.reshape(across_px, members, rows, width))
    outs = chain.run(
        "x_pass",
        kernel,
        args,
        in_specs,
        out_specs,
        out_shape,
        grid=(steps * members,),
        scratch=[pltpu.VMEM((length, fields * width), jnp.bfloat16)],
        flops=6 * length * length * width * fields,
        limit=MOST_VMEM_BYTES,
    )
    return [outs[n * members : (n + 1) * members] for n in range(fields)], outs[-1] if first else speed


def y_pass(chain, which, operators, viscosity, parts, speed, yb, shape, block):
    across_px, rows, width = parts[0][0].shape
    fields, members = len(parts), len(parts[0])
    part = yb // members
    length = width * members
    blocks = length // yb
    height = across_px * rows
    first = which[0] == V

    def kernel(at, visc_ref, op_ref, *refs):
        part_refs, rest = refs[: fields * members], refs[fields * members :]
        if first:
            out, speed_ref, lines = rest
        else:
            speed_ref, out, lines = rest
        step = pl.program_id(0)

        @pl.when(step == 0)
        def _():
            for n in range(fields):
                for r in range(members):
                    values = part_refs[n * members + r][...].reshape(height, width)
                    if in_order(part):
                        for y in range(blocks):
                            start = pl.multiple_of(y * yb + (at[1] ^ r) * part, part)
                            lines[n, :, pl.ds(start, part)] = values[:, y * part : (y + 1) * part]
                    else:
                        start = pl.multiple_of((at[1] ^ r) * width, width)
                        lines[n, :, pl.ds(start, width)] = values
            if first:
                for y in range(blocks):
                    if in_order(part):
                        speed_ref[y] = lines[0, :, y * yb : (y + 1) * yb]
                    else:
                        for k in range(members):
                            start = k * width + y * part
                            speed_ref[y, :, k * part : (k + 1) * part] = lines[0, :, start : start + part]

        v = speed_ref[step if first else 0].astype(jnp.float32)
        for n, field in enumerate(which):
            result = lax.dot_general(
                lines[n],
                op_ref[...].reshape(3 * yb, length),
                (((1,), (1,)), ((), ())),
                preferred_element_type=jnp.float32,
            )
            value = result[:, 2 * yb :] + time_step * (
                -v * result[:, :yb] + visc_ref[field] * result[:, yb : 2 * yb]
            )
            value = value.astype(jnp.bfloat16)
            if len(which) == 1:
                out[...] = value.reshape(block)
            else:
                out[0, :, n] = value.reshape(across_px, rows, yb)

    flat = [part for field_parts in parts for part in field_parts]
    in_specs = [smem, pl.BlockSpec((3, yb, length), lambda i, at: (0, i, 0))] + like(flat)
    args = [viscosity, operators, *flat]
    out_specs = [pl.BlockSpec(block, lambda i, at: (i,) + (0,) * (len(block) - 1))]
    out_shape = [jax.ShapeDtypeStruct(shape, jnp.bfloat16)]
    if first:
        out_specs.append(whole((blocks, height, yb)))
        out_shape.append(jax.ShapeDtypeStruct((blocks, height, yb), jnp.bfloat16))
    else:
        in_specs.append(pl.BlockSpec((1, height, yb), lambda i, at: (i, 0, 0)))
        args.append(speed)
    outs = chain.run(
        "y_pass",
        kernel,
        args,
        in_specs,
        out_specs,
        out_shape,
        grid=(blocks,),
        scratch=[pltpu.VMEM((fields, height, length), jnp.bfloat16)],
        flops=6 * length * length * height * fields,
        limit=MOST_VMEM_BYTES,
    )
    return outs[0], outs[1] if first else speed


def put(chain, buffer, arrived, which, block, shape):
    across_py, across_px = arrived.shape[:2]
    extra = [] if buffer is None else [buffer]
    many = len(which)
    first, stride = which[0], which[1] - which[0] if many > 1 else 0

    def kernel(at, arrived_ref, *refs):
        refs[-1][...] = arrived_ref[...].reshape(refs[-1].shape)

    return chain.run(
        "put",
        kernel,
        [arrived, *extra],
        [pl.BlockSpec((across_py, across_px, block) + arrived.shape[3:], lambda n, at: (0, 0, n, 0, 0))]
        + [anywhere] * len(extra),
        [pl.BlockSpec((1,) + shape[1:], lambda n, at: (first + n * stride, 0, 0, 0))],
        [jax.ShapeDtypeStruct(shape, arrived.dtype)],
        grid=(many,),
        aliases={2: 0} if extra else {},
        limit=SMALL_VMEM_BYTES,
        free=True,
    )[0]


def wall_lines(chain, arrived, n, tile, slot, buffer):
    across_py, across_px, _, rows, yb = arrived.shape
    count, span = tile.shape[0], across_px * across_py * rows
    devices = across_px * across_py
    units, unit = buffer.shape[2:4]

    def kernel(at, tile_ref, slot_ref, arrived_ref, buffer_ref, out):
        chosen = tile_ref[...] == lax.broadcasted_iota(jnp.int32, (count, span), 1)
        flux = jnp.dot(
            chosen.astype(jnp.float32).astype(jnp.bfloat16),
            arrived_ref[...].reshape(span, yb),
            preferred_element_type=jnp.float32,
        )
        filled = slot_ref[...] == lax.broadcasted_iota(jnp.int32, (devices * unit, count), 0)
        out[...] = (
            jnp.dot(
                filled.astype(jnp.float32).astype(jnp.bfloat16),
                flux.astype(jnp.bfloat16),
                preferred_element_type=jnp.float32,
            )
            .astype(jnp.bfloat16)
            .reshape(across_py, across_px, 1, unit, yb)
        )

    args = [tile.reshape(-1, 1), slot.reshape(1, -1)]
    return chain.run(
        "wall_lines",
        kernel,
        args + [arrived, buffer],
        like(args)
        + [pl.BlockSpec((across_py, across_px, 1, rows, yb), lambda i, at: (0, 0, n, 0, 0)), anywhere],
        [pl.BlockSpec((across_py, across_px, 1, unit, yb), lambda i, at: (0, 0, units - 1, 0, 0))],
        [jax.ShapeDtypeStruct(buffer.shape, buffer.dtype)],
        aliases={4: 0},
        limit=SMALL_VMEM_BYTES,
    )[0]


def add_flux(chain, tags, arrived, solid_temp, conductivity):
    rows, columns = solid_temp.shape
    across_py, across_px, units, unit, _ = arrived.shape

    def kernel(at, temp_ref, kappa_ref, arrived_ref, *refs):
        tag_refs, out = refs[:-1], refs[-1]
        out[0] = temp_ref[...]
        out[1] = kappa_ref[...]
        places = lax.broadcasted_iota(jnp.int32, (rows, unit), 0)
        source = jnp.zeros((rows, columns), jnp.float32)
        for s in range(across_py):
            chosen = [tag_refs[s][at[7] ^ t] == places for t in range(across_px)]
            chosen = jnp.concatenate([c.astype(jnp.float32) for c in chosen], axis=1)
            source = source + jnp.dot(
                chosen.astype(jnp.bfloat16),
                arrived_ref[at[2] ^ s].reshape(across_px * unit, columns),
                preferred_element_type=jnp.float32,
            )
        out[2] = (wall_gain * source_gain) * source

    args = [solid_temp, conductivity]
    lines = pl.BlockSpec(
        (across_py, across_px, 1, unit, columns), lambda i, at: (0, 0, units - 1, 0, 0)
    )
    return chain.run(
        "add_flux",
        kernel,
        args + [arrived, *tags],
        like(args) + [lines] + like(tags),
        [whole((3, rows, columns))],
        [jax.ShapeDtypeStruct((3, rows, columns), jnp.float32)],
    )[0]


def conduct_and_put(chain, solid, low, high, margin, buffer, arrived, field):
    across_py, across_px, _, x_rows, _ = arrived.shape
    members = buffer.shape[2] // x_rows
    groups = across_px // members
    kinds, height, columns = solid.shape
    rows = height - 2 * margin
    wide = columns + -(-2 * margin // 128) * 128

    def kernel(at, solid_ref, low_ref, high_ref, arrived_ref, buffer_ref, out, fields_ref, ext, sems):
        copies = [
            pltpu.make_async_copy(
                arrived_ref.at[k, a, 0],
                fields_ref.at[field, k * groups + a // members, pl.ds(a % members * x_rows, x_rows)],
                sems.at[k, a],
            )
            for k in range(across_py)
            for a in range(across_px)
        ]
        for copy in copies:
            copy.start()
        ext[:, :, columns:] = jnp.zeros((kinds, height, wide - columns), jnp.float32)
        ext[:, :, :columns] = solid_ref[...]
        ext[:, :, columns : columns + margin] = high_ref[...]
        ext[:, :, wide - margin :] = low_ref[...]
        t, kappa, heat = ext[0], ext[1], ext[2]
        row = lax.broadcasted_iota(jnp.int32, (height, wide), 0) + at[3]
        col = lax.broadcasted_iota(jnp.int32, (height, wide), 1)
        col = jnp.where(col < wide - margin, col, col - wide) + at[4]
        inside = (row >= 0) & (row < at[5]) & (col >= 0) & (col < at[6])
        moves = ((height - 1, 0), (1, 0), (wide - 1, 1), (1, 1))
        faces = [
            jnp.where(inside, diffusion_rate * 0.5 * (kappa + pltpu.roll(kappa, shift, dim)), 0.0)
            for shift, dim in moves
        ]
        for _ in range(COND_STEPS):
            change = heat
            for face, (shift, dim) in zip(faces, moves):
                change = change + face * (pltpu.roll(t, shift, dim) - t)
            t = t + change
        out[...] = t[margin : margin + rows, :columns]
        for copy in copies:
            copy.wait()

    args = [solid, low, high, arrived]
    return chain.run(
        "conduct_and_put",
        kernel,
        args + [buffer],
        like(args) + [anywhere],
        [whole((rows, columns)), anywhere],
        [
            jax.ShapeDtypeStruct((rows, columns), jnp.float32),
            jax.ShapeDtypeStruct(buffer.shape, buffer.dtype),
        ],
        scratch=[
            pltpu.VMEM((kinds, height, wide), jnp.float32),
            pltpu.SemaphoreType.DMA((across_py, across_px)),
        ],
        aliases={5: 1},
        limit=SMALL_VMEM_BYTES,
    )


def on_device(
    fields,
    x_operators,
    y_operators,
    viscosity,
    wall_tile,
    wall_owner,
    wall_row,
    solid_temp,
    conductivity,
):
    across_px, across_py = lax.axis_size("px"), lax.axis_size("py")
    devices = across_px * across_py
    layers, xb, yb = fields.shape[1:]
    groups = layers // across_py
    members = across_px // groups
    a, b = lax.axis_index("px"), lax.axis_index("py")
    q, m = a // members, a % members
    rows, columns = solid_temp.shape
    margin = COND_STEPS
    at = jnp.stack(
        [
            q,
            m,
            b,
            a * rows - margin,
            b * columns,
            across_px * rows,
            across_py * columns,
            a,
        ]
    ).astype(jnp.int32)
    chain = Chain(at)

    def along(axis, pieces):
        return [pieces[0]] + [
            lax.ppermute(piece, axis, [(i, i ^ s) for i in range(lax.axis_size(axis))])
            for s, piece in enumerate(pieces[1:], 1)
        ]

    def exchange(blocks):
        moved = lax.all_to_all(
            blocks.reshape((devices,) + blocks.shape[2:]),
            ("py", "px"),
            split_axis=0,
            concat_axis=0,
            tiled=True,
        )
        return moved.reshape(blocks.shape)

    half, speeds = {}, {}

    def forward(*which):
        return exchange(cut(chain, fields, which, across_px, across_py))

    def X(arrived, *which):
        outs, speeds[U] = x_pass(
            chain, which, x_operators, viscosity, arrived, members, speeds.get(U)
        )
        for f, out in zip(which, outs):
            half[f] = along("px", out)

    y_columns = y_operators
    if not in_order(yb // members):
        y_columns = y_columns.reshape(3, -1, across_py, members, yb // members)
        y_columns = y_columns.swapaxes(2, 3).reshape(y_operators.shape)

    x_rows = xb // members
    unit = min(16, x_rows)

    def Y(*which, slots=False):
        shape = (across_py, across_px, len(which), x_rows, yb)
        block = (1,) + shape[1:]
        if slots:
            shape = (across_py, across_px, x_rows // unit + 1, unit, yb)
            block = (1, across_px, x_rows // unit, unit, yb)
        out, speeds[V] = y_pass(
            chain,
            which,
            y_columns,
            viscosity,
            [half[f] for f in which],
            speeds.get(V),
            yb,
            shape,
            block,
        )
        return out

    most = forward(U, V, THETA)

    count = wall_tile.shape[0]
    owner = wall_owner[:, 0]
    capacity = max(2, 4 * count // devices)
    assert capacity <= unit
    order = jnp.arange(count, dtype=jnp.int32)
    earlier = (owner[:, None] == owner[None, :]) & (order[None, :] < order[:, None])
    position = jnp.sum(earlier.astype(jnp.int32), axis=1)
    label = owner * unit + position
    filled = label[None, :] == jnp.arange(devices * unit, dtype=jnp.int32)[:, None]
    labels = jnp.sum(jnp.where(filled, wall_row[None, :] + 1, 0), axis=1) - 1
    labels = labels.reshape(across_px, across_py, unit)
    slot = (owner % across_py * across_px + owner // across_py) * unit + position
    tags = along(
        "px",
        [lax.dynamic_index_in_dim(labels, a ^ s, 0, keepdims=False) for s in range(across_px)],
    )
    chain.last += tags
    last = forward(W)
    tags = along(
        "py",
        [
            jnp.stack([lax.dynamic_index_in_dim(tag, b ^ s, 0) for tag in tags])
            for s in range(across_py)
        ],
    )

    chain.last += tags
    X(most, U, V, THETA)
    first = exchange(Y(V, THETA))
    second = Y(U, slots=True)
    X(last, W)
    third = Y(W)
    second = exchange(wall_lines(chain, first, 1, wall_tile, slot, second))
    third = exchange(third)
    new_fields = put(chain, None, first, (V, THETA), 1, fields.shape)
    solid = add_flux(chain, tags, second, solid_temp, conductivity)
    low, high = margins(solid, "px", 1, margin)
    solid = jnp.concatenate([low, solid, high], axis=1)
    new_fields = put(chain, new_fields, second, (U,), x_rows // unit, fields.shape)
    low, high = margins(solid, "py", 2, margin)
    new_solid, new_fields = conduct_and_put(
        chain, solid, low, high, margin, new_fields, third, W
    )
    return new_fields, new_solid


def solution(mesh):
    return jax.shard_map(
        on_device,
        mesh=mesh,
        in_specs=(
            P(None, None, "px", "py"),
            P(),
            P(),
            P(),
            P(("px", "py")),
            P(("px", "py"), None),
            P(("px", "py")),
            P("px", "py"),
            P("px", "py"),
        ),
        out_specs=(P(None, None, "px", "py"), P("px", "py")),
        check_vma=False,
    )
```

```python
import jax
import jax.numpy as jnp
from jax import lax
from jax.experimental import pallas as pl
from jax.experimental.pallas import tpu as pltpu
from jax.sharding import PartitionSpec as P

COND_STEPS = 8

time_step = 0.25
wall_gain = 0.5
diffusion_rate = 0.24
source_gain = 0.1

U, V, W, THETA = 0, 1, 2, 3
SMALL_VMEM_BYTES = 16 * 1024 * 1024
MOST_VMEM_BYTES = 56 * 1024 * 1024

smem = pl.BlockSpec(memory_space=pltpu.SMEM)
anywhere = pl.BlockSpec(memory_space=pl.ANY)


def margins(block, axis, dim, width):
    count = lax.axis_size(axis)
    forward = [(i, i + 1) for i in range(count - 1)]
    backward = [(target, source) for source, target in forward]
    low = lax.ppermute(
        lax.slice_in_dim(block, block.shape[dim] - width, None, axis=dim), axis, forward
    )
    high = lax.ppermute(lax.slice_in_dim(block, 0, width, axis=dim), axis, backward)
    return low, high


def in_order(part):
    return part % 128 == 0


class Chain:
    def __init__(self, at):
        self.at = at
        self.last = []

    def run(
        self,
        name,
        kernel,
        args,
        in_specs,
        out_specs,
        out_shape,
        grid=(1,),
        scratch=(),
        aliases=None,
        flops=0,
        limit=MOST_VMEM_BYTES,
        free=False,
    ):
        count = len(args)
        tokens = [] if free else [x for x in self.last if not any(x is y for y in args)]

        def body(at_ref, *refs):
            kernel(at_ref, *refs[:count], *refs[count + len(tokens) :])

        moved = sum(x.size * x.dtype.itemsize for x in out_shape)
        outs = pl.pallas_call(
            body,
            grid_spec=pltpu.PrefetchScalarGridSpec(
                num_scalar_prefetch=1,
                grid=grid,
                in_specs=list(in_specs) + [anywhere] * len(tokens),
                out_specs=out_specs,
                scratch_shapes=list(scratch),
            ),
            out_shape=out_shape,
            input_output_aliases=aliases or {},
            compiler_params=pltpu.CompilerParams(vmem_limit_bytes=limit),
            cost_estimate=pl.CostEstimate(flops=flops, bytes_accessed=2 * moved, transcendentals=0),
            name=name,
        )(self.at, *args, *tokens)
        if not free:
            self.last = [min(outs, key=lambda x: x.size)]
        return outs


def whole(shape):
    return pl.BlockSpec(shape, lambda i, at: (0,) * len(shape))


def like(pieces):
    return [whole(piece.shape) for piece in pieces]


def cut(chain, fields, which, across_px, across_py):
    layers, xb, yb = fields.shape[1:]
    groups = layers // across_py
    members = across_px // groups
    part = yb // members
    many = len(which)
    shape = (across_py, groups, members, many, xb, part)

    def copying(at, fields_ref, out, held, arrived, left):
        loads = [
            [
                pltpu.make_async_copy(
                    fields_ref.at[f, pl.ds(y * groups, groups), :, pl.ds(k * part, part)],
                    held.at[y, :, k, n],
                    arrived.at[y, k, n],
                )
                for k in range(members)
                for n, f in enumerate(which)
            ]
            for y in range(across_py)
        ]
        stores = [
            pltpu.make_async_copy(held.at[y], out.at[y], left.at[y]) for y in range(across_py)
        ]
        for block in loads:
            for copy in block:
                copy.start()
        for block, store in zip(loads, stores):
            for copy in block:
                copy.wait()
            store.start()
        for store in stores:
            store.wait()

    def slicing(at, *refs):
        for n in range(many):
            for k in range(members):
                refs[-1][0, :, k, n] = refs[n][0, :, :, k * part : (k + 1) * part]

    def field(f):
        return pl.BlockSpec((1, groups, xb, yb), lambda i, at: (f, i, 0, 0))

    if in_order(part):
        out = chain.run(
            "cut",
            copying,
            [fields],
            [anywhere],
            [anywhere],
            [jax.ShapeDtypeStruct(shape, fields.dtype)],
            scratch=[
                pltpu.VMEM(shape, fields.dtype),
                pltpu.SemaphoreType.DMA((across_py, members, many)),
                pltpu.SemaphoreType.DMA((across_py,)),
            ],
        )[0]
    else:
        out = chain.run(
            "cut",
            slicing,
            [fields] * many,
            [field(f) for f in which],
            [pl.BlockSpec((1,) + shape[1:], lambda i, at: (i, 0, 0, 0, 0, 0))],
            [jax.ShapeDtypeStruct(shape, fields.dtype)],
            grid=(across_py,),
            limit=SMALL_VMEM_BYTES,
        )[0]
    return out.reshape((across_py, across_px) + shape[3:])


def x_pass(chain, which, operators, viscosity, arrived, at_fields, members, speed):
    across_py, across_px, held, xb, part = arrived.shape
    fields = len(which)
    width = across_py * part
    length = across_px * xb
    rows = xb // members
    many = min(across_px, max(1, 256 // rows))
    steps = across_px // many
    first = speed is None
    only = fields == 1

    def kernel(at, visc_ref, op_ref, arrived_ref, *refs):
        speed_ref, outs, lines = refs[0], refs[1:-1], refs[-1]
        if first:
            speed_ref, outs = refs[-2], refs[:-2]
        step = pl.program_id(0)
        turn, place = step // steps, step % steps

        @pl.when(step == 0)
        def _():
            for x in range(across_px):
                rows_of = slice(x * xb, (x + 1) * xb)
                for y in range(across_py):
                    for n, field in enumerate(which):
                        start = n * width + y * part
                        piece = arrived_ref[y, x, 0 if only else at_fields.index(field)]
                        lines[rows_of, start : start + part] = piece
                    if first:
                        piece = arrived_ref[y, x, at_fields.index(U)]
                        speed_ref[rows_of, y * part : (y + 1) * part] = piece

        block = op_ref[...].reshape(3 * many * rows, length)
        whole_result = jnp.dot(block, lines[...], preferred_element_type=jnp.float32)
        for n, field in enumerate(which):
            result = whole_result[:, n * width : (n + 1) * width].reshape(3, many, rows, width)
            for c in range(many):
                if first:
                    row = (place * many + c) * xb + (at[1] ^ turn) * rows
                    u = speed_ref[pl.ds(pl.multiple_of(row, rows), rows), :]
                else:
                    u = speed_ref[c, 0]
                value = result[2, c] + time_step * (
                    -u.astype(jnp.float32) * result[0, c] + visc_ref[field] * result[1, c]
                )
                value = value.astype(jnp.bfloat16)
                for r in range(members):

                    @pl.when(turn == r)
                    def _():
                        outs[n * members + r][c] = value

    def out_block(r):
        return pl.BlockSpec(
            (many, rows, width), lambda i, at: (jnp.clip(i - r * steps, 0, steps - 1), 0, 0)
        )

    def place_of(i, at):
        return i % steps, at[1] ^ (i // steps), 0, 0

    in_specs = [
        smem,
        pl.BlockSpec((3, many, 1, rows, length), lambda i, at: (0,) + place_of(i, at)),
        pl.BlockSpec(
            (across_py, across_px, 1 if only else held, xb, part),
            lambda i, at: (0, 0, at_fields.index(which[0]) if only else 0, 0, 0),
        ),
    ]
    args = [viscosity, operators.reshape(3, across_px, members, rows, length), arrived]
    out_specs = [out_block(r) for _ in which for r in range(members)]
    out_shape = [jax.ShapeDtypeStruct((across_px, rows, width), jnp.bfloat16)] * len(out_specs)
    if first:
        out_specs.append(whole((length, width)))
        out_shape.append(jax.ShapeDtypeStruct((length, width), jnp.bfloat16))
    else:
        in_specs.append(pl.BlockSpec((many, 1, rows, width), place_of))
        args.append(speed.reshape(across_px, members, rows, width))
    outs = chain.run(
        "x_pass",
        kernel,
        args,
        in_specs,
        out_specs,
        out_shape,
        grid=(steps * members,),
        scratch=[pltpu.VMEM((length, fields * width), jnp.bfloat16)],
        flops=6 * length * length * width * fields,
        limit=MOST_VMEM_BYTES,
    )
    return [outs[n * members : (n + 1) * members] for n in range(fields)], outs[-1] if first else speed


def y_pass(chain, which, operators, viscosity, parts, speed, yb, shape, block):
    across_px, rows, width = parts[0][0].shape
    fields, members = len(parts), len(parts[0])
    part = yb // members
    length = width * members
    blocks = length // yb
    height = across_px * rows
    first = which[0] == V

    def kernel(at, visc_ref, op_ref, *refs):
        part_refs, rest = refs[: fields * members], refs[fields * members :]
        if first:
            out, speed_ref, lines = rest
        else:
            speed_ref, out, lines = rest
        step = pl.program_id(0)

        @pl.when(step == 0)
        def _():
            for n in range(fields):
                for r in range(members):
                    values = part_refs[n * members + r][...].reshape(height, width)
                    if in_order(part):
                        for y in range(blocks):
                            start = pl.multiple_of(y * yb + (at[1] ^ r) * part, part)
                            lines[n, :, pl.ds(start, part)] = values[:, y * part : (y + 1) * part]
                    else:
                        start = pl.multiple_of((at[1] ^ r) * width, width)
                        lines[n, :, pl.ds(start, width)] = values
            if first:
                for y in range(blocks):
                    if in_order(part):
                        speed_ref[y] = lines[0, :, y * yb : (y + 1) * yb]
                    else:
                        for k in range(members):
                            start = k * width + y * part
                            speed_ref[y, :, k * part : (k + 1) * part] = lines[0, :, start : start + part]

        v = speed_ref[step if first else 0].astype(jnp.float32)
        whole_result = lax.dot_general(
            lines[...].reshape(fields * height, length),
            op_ref[...].reshape(3 * yb, length),
            (((1,), (1,)), ((), ())),
            preferred_element_type=jnp.float32,
        )
        for n, field in enumerate(which):
            result = whole_result[n * height : (n + 1) * height]
            value = result[:, 2 * yb :] + time_step * (
                -v * result[:, :yb] + visc_ref[field] * result[:, yb : 2 * yb]
            )
            value = value.astype(jnp.bfloat16)
            if len(which) == 1:
                out[...] = value.reshape(block)
            else:
                out[0, :, n] = value.reshape(across_px, rows, yb)

    flat = [part for field_parts in parts for part in field_parts]
    in_specs = [smem, pl.BlockSpec((3, yb, length), lambda i, at: (0, i, 0))] + like(flat)
    args = [viscosity, operators, *flat]
    out_specs = [pl.BlockSpec(block, lambda i, at: (i,) + (0,) * (len(block) - 1))]
    out_shape = [jax.ShapeDtypeStruct(shape, jnp.bfloat16)]
    if first:
        out_specs.append(whole((blocks, height, yb)))
        out_shape.append(jax.ShapeDtypeStruct((blocks, height, yb), jnp.bfloat16))
    else:
        in_specs.append(pl.BlockSpec((1, height, yb), lambda i, at: (i, 0, 0)))
        args.append(speed)
    outs = chain.run(
        "y_pass",
        kernel,
        args,
        in_specs,
        out_specs,
        out_shape,
        grid=(blocks,),
        scratch=[pltpu.VMEM((fields, height, length), jnp.bfloat16)],
        flops=6 * length * length * height * fields,
        limit=MOST_VMEM_BYTES,
    )
    return outs[0], outs[1] if first else speed


def put(chain, buffer, arrived, which, block, shape):
    across_py, across_px = arrived.shape[:2]
    extra = [] if buffer is None else [buffer]
    many = len(which)
    first, stride = which[0], which[1] - which[0] if many > 1 else 0

    def kernel(at, arrived_ref, *refs):
        refs[-1][...] = arrived_ref[...].reshape(refs[-1].shape)

    return chain.run(
        "put",
        kernel,
        [arrived, *extra],
        [pl.BlockSpec((across_py, across_px, block) + arrived.shape[3:], lambda n, at: (0, 0, n, 0, 0))]
        + [anywhere] * len(extra),
        [pl.BlockSpec((1,) + shape[1:], lambda n, at: (first + n * stride, 0, 0, 0))],
        [jax.ShapeDtypeStruct(shape, arrived.dtype)],
        grid=(many,),
        aliases={2: 0} if extra else {},
        limit=SMALL_VMEM_BYTES,
        free=True,
    )[0]


def wall_lines(chain, arrived, n, tile, slot, buffer):
    across_py, across_px, _, rows, yb = arrived.shape
    count, span = tile.shape[0], across_px * across_py * rows
    devices = across_px * across_py
    units, unit = buffer.shape[2:4]

    def kernel(at, tile_ref, slot_ref, arrived_ref, buffer_ref, out):
        chosen = tile_ref[...] == lax.broadcasted_iota(jnp.int32, (count, span), 1)
        flux = jnp.dot(
            chosen.astype(jnp.float32).astype(jnp.bfloat16),
            arrived_ref[...].reshape(span, yb),
            preferred_element_type=jnp.float32,
        )
        filled = slot_ref[...] == lax.broadcasted_iota(jnp.int32, (devices * unit, count), 0)
        out[...] = (
            jnp.dot(
                filled.astype(jnp.float32).astype(jnp.bfloat16),
                flux.astype(jnp.bfloat16),
                preferred_element_type=jnp.float32,
            )
            .astype(jnp.bfloat16)
            .reshape(across_py, across_px, 1, unit, yb)
        )

    args = [tile.reshape(-1, 1), slot.reshape(1, -1)]
    return chain.run(
        "wall_lines",
        kernel,
        args + [arrived, buffer],
        like(args)
        + [pl.BlockSpec((across_py, across_px, 1, rows, yb), lambda i, at: (0, 0, n, 0, 0)), anywhere],
        [pl.BlockSpec((across_py, across_px, 1, unit, yb), lambda i, at: (0, 0, units - 1, 0, 0))],
        [jax.ShapeDtypeStruct(buffer.shape, buffer.dtype)],
        aliases={4: 0},
        limit=SMALL_VMEM_BYTES,
    )[0]


def add_flux(chain, tags, arrived, solid_temp, conductivity):
    rows, columns = solid_temp.shape
    across_py, across_px, units, unit, _ = arrived.shape

    def kernel(at, temp_ref, kappa_ref, arrived_ref, *refs):
        tag_refs, out = refs[:-1], refs[-1]
        out[0] = temp_ref[...]
        out[1] = kappa_ref[...]
        places = lax.broadcasted_iota(jnp.int32, (rows, unit), 0)
        source = jnp.zeros((rows, columns), jnp.float32)
        for s in range(across_py):
            chosen = [tag_refs[s][at[7] ^ t] == places for t in range(across_px)]
            chosen = jnp.concatenate([c.astype(jnp.float32) for c in chosen], axis=1)
            source = source + jnp.dot(
                chosen.astype(jnp.bfloat16),
                arrived_ref[at[2] ^ s].reshape(across_px * unit, columns),
                preferred_element_type=jnp.float32,
            )
        out[2] = (wall_gain * source_gain) * source

    args = [solid_temp, conductivity]
    lines = pl.BlockSpec(
        (across_py, across_px, 1, unit, columns), lambda i, at: (0, 0, units - 1, 0, 0)
    )
    return chain.run(
        "add_flux",
        kernel,
        args + [arrived, *tags],
        like(args) + [lines] + like(tags),
        [whole((3, rows, columns))],
        [jax.ShapeDtypeStruct((3, rows, columns), jnp.float32)],
    )[0]


def conduct_and_put(chain, solid, low, high, margin, buffer, arrived, field):
    across_py, across_px, _, x_rows, _ = arrived.shape
    members = buffer.shape[2] // x_rows
    groups = across_px // members
    kinds, height, columns = solid.shape
    rows = height - 2 * margin
    wide = columns + -(-2 * margin // 128) * 128

    def kernel(at, solid_ref, low_ref, high_ref, arrived_ref, buffer_ref, out, fields_ref, ext, sems):
        copies = [
            pltpu.make_async_copy(
                arrived_ref.at[k, a, 0],
                fields_ref.at[field, k * groups + a // members, pl.ds(a % members * x_rows, x_rows)],
                sems.at[k, a],
            )
            for k in range(across_py)
            for a in range(across_px)
        ]
        for copy in copies:
            copy.start()
        ext[:, :, columns:] = jnp.zeros((kinds, height, wide - columns), jnp.float32)
        ext[:, :, :columns] = solid_ref[...]
        ext[:, :, columns : columns + margin] = high_ref[...]
        ext[:, :, wide - margin :] = low_ref[...]
        t, kappa, heat = ext[0], ext[1], ext[2]
        row = lax.broadcasted_iota(jnp.int32, (height, wide), 0) + at[3]
        col = lax.broadcasted_iota(jnp.int32, (height, wide), 1)
        col = jnp.where(col < wide - margin, col, col - wide) + at[4]
        inside = (row >= 0) & (row < at[5]) & (col >= 0) & (col < at[6])
        moves = ((height - 1, 0), (1, 0), (wide - 1, 1), (1, 1))
        faces = [
            jnp.where(inside, diffusion_rate * 0.5 * (kappa + pltpu.roll(kappa, shift, dim)), 0.0)
            for shift, dim in moves
        ]
        for _ in range(COND_STEPS):
            change = heat
            for face, (shift, dim) in zip(faces, moves):
                change = change + face * (pltpu.roll(t, shift, dim) - t)
            t = t + change
        out[...] = t[margin : margin + rows, :columns]
        for copy in copies:
            copy.wait()

    args = [solid, low, high, arrived]
    return chain.run(
        "conduct_and_put",
        kernel,
        args + [buffer],
        like(args) + [anywhere],
        [whole((rows, columns)), anywhere],
        [
            jax.ShapeDtypeStruct((rows, columns), jnp.float32),
            jax.ShapeDtypeStruct(buffer.shape, buffer.dtype),
        ],
        scratch=[
            pltpu.VMEM((kinds, height, wide), jnp.float32),
            pltpu.SemaphoreType.DMA((across_py, across_px)),
        ],
        aliases={5: 1},
        limit=SMALL_VMEM_BYTES,
    )


def on_device(
    fields,
    x_operators,
    y_operators,
    viscosity,
    wall_tile,
    wall_owner,
    wall_row,
    solid_temp,
    conductivity,
):
    across_px, across_py = lax.axis_size("px"), lax.axis_size("py")
    devices = across_px * across_py
    layers, xb, yb = fields.shape[1:]
    groups = layers // across_py
    members = across_px // groups
    a, b = lax.axis_index("px"), lax.axis_index("py")
    q, m = a // members, a % members
    rows, columns = solid_temp.shape
    margin = COND_STEPS
    at = jnp.stack(
        [
            q,
            m,
            b,
            a * rows - margin,
            b * columns,
            across_px * rows,
            across_py * columns,
            a,
        ]
    ).astype(jnp.int32)
    chain = Chain(at)

    def along(axis, pieces):
        return [pieces[0]] + [
            lax.ppermute(piece, axis, [(i, i ^ s) for i in range(lax.axis_size(axis))])
            for s, piece in enumerate(pieces[1:], 1)
        ]

    def exchange(blocks):
        moved = lax.all_to_all(
            blocks.reshape((devices,) + blocks.shape[2:]),
            ("py", "px"),
            split_axis=0,
            concat_axis=0,
            tiled=True,
        )
        return moved.reshape(blocks.shape)

    half, speeds = {}, {}

    def forward(*which):
        return exchange(cut(chain, fields, which, across_px, across_py))

    def X(arrived, at_fields, *which):
        outs, speeds[U] = x_pass(
            chain, which, x_operators, viscosity, arrived, at_fields, members, speeds.get(U)
        )
        for f, out in zip(which, outs):
            half[f] = along("px", out)

    y_columns = y_operators
    if not in_order(yb // members):
        y_columns = y_columns.reshape(3, -1, across_py, members, yb // members)
        y_columns = y_columns.swapaxes(2, 3).reshape(y_operators.shape)

    x_rows = xb // members
    unit = min(16, x_rows)

    def Y(*which, slots=False):
        shape = (across_py, across_px, len(which), x_rows, yb)
        block = (1,) + shape[1:]
        if slots:
            shape = (across_py, across_px, x_rows // unit + 1, unit, yb)
            block = (1, across_px, x_rows // unit, unit, yb)
        out, speeds[V] = y_pass(
            chain,
            which,
            y_columns,
            viscosity,
            [half[f] for f in which],
            speeds.get(V),
            yb,
            shape,
            block,
        )
        return out

    most = forward(U, V, THETA)

    count = wall_tile.shape[0]
    owner = wall_owner[:, 0]
    capacity = max(2, 4 * count // devices)
    assert capacity <= unit
    order = jnp.arange(count, dtype=jnp.int32)
    earlier = (owner[:, None] == owner[None, :]) & (order[None, :] < order[:, None])
    position = jnp.sum(earlier.astype(jnp.int32), axis=1)
    label = owner * unit + position
    filled = label[None, :] == jnp.arange(devices * unit, dtype=jnp.int32)[:, None]
    labels = jnp.sum(jnp.where(filled, wall_row[None, :] + 1, 0), axis=1) - 1
    labels = labels.reshape(across_px, across_py, unit)
    slot = (owner % across_py * across_px + owner // across_py) * unit + position
    tags = along(
        "px",
        [lax.dynamic_index_in_dim(labels, a ^ s, 0, keepdims=False) for s in range(across_px)],
    )
    chain.last += tags
    last = forward(W)
    tags = along(
        "py",
        [
            jnp.stack([lax.dynamic_index_in_dim(tag, b ^ s, 0) for tag in tags])
            for s in range(across_py)
        ],
    )

    X(most, (U, V, THETA), V, THETA)
    first = exchange(Y(V, THETA))
    X(most, (U, V, THETA), U)
    second = Y(U, slots=True)
    X(last, (W,), W)
    third = Y(W)
    chain.last += tags
    second = exchange(wall_lines(chain, first, 1, wall_tile, slot, second))
    third = exchange(third)
    new_fields = put(chain, None, first, (V, THETA), 1, fields.shape)
    solid = add_flux(chain, tags, second, solid_temp, conductivity)
    low, high = margins(solid, "px", 1, margin)
    solid = jnp.concatenate([low, solid, high], axis=1)
    new_fields = put(chain, new_fields, second, (U,), x_rows // unit, fields.shape)
    low, high = margins(solid, "py", 2, margin)
    new_solid, new_fields = conduct_and_put(
        chain, solid, low, high, margin, new_fields, third, W
    )
    return new_fields, new_solid


def solution(mesh):
    return jax.shard_map(
        on_device,
        mesh=mesh,
        in_specs=(
            P(None, None, "px", "py"),
            P(),
            P(),
            P(),
            P(("px", "py")),
            P(("px", "py"), None),
            P(("px", "py")),
            P("px", "py"),
            P("px", "py"),
        ),
        out_specs=(P(None, None, "px", "py"), P("px", "py")),
        check_vma=False,
    )
```

```python
import jax
import jax.numpy as jnp
from jax import lax
from jax.experimental import pallas as pl
from jax.experimental.pallas import tpu as pltpu
from jax.sharding import PartitionSpec as P

COND_STEPS = 8

time_step = 0.25
wall_gain = 0.5
diffusion_rate = 0.24
source_gain = 0.1

U, V, W, THETA = 0, 1, 2, 3
SMALL_VMEM_BYTES = 16 * 1024 * 1024
MOST_VMEM_BYTES = 56 * 1024 * 1024

smem = pl.BlockSpec(memory_space=pltpu.SMEM)
anywhere = pl.BlockSpec(memory_space=pl.ANY)


def margins(block, axis, dim, width):
    count = lax.axis_size(axis)
    forward = [(i, i + 1) for i in range(count - 1)]
    backward = [(target, source) for source, target in forward]
    low = lax.ppermute(
        lax.slice_in_dim(block, block.shape[dim] - width, None, axis=dim), axis, forward
    )
    high = lax.ppermute(lax.slice_in_dim(block, 0, width, axis=dim), axis, backward)
    return low, high


def in_order(part):
    return part % 128 == 0


class Chain:
    def __init__(self, at):
        self.at = at
        self.last = []

    def run(
        self,
        name,
        kernel,
        args,
        in_specs,
        out_specs,
        out_shape,
        grid=(1,),
        scratch=(),
        aliases=None,
        flops=0,
        limit=MOST_VMEM_BYTES,
        free=False,
    ):
        count = len(args)
        tokens = [] if free else [x for x in self.last if not any(x is y for y in args)]

        def body(at_ref, *refs):
            kernel(at_ref, *refs[:count], *refs[count + len(tokens) :])

        moved = sum(x.size * x.dtype.itemsize for x in out_shape)
        outs = pl.pallas_call(
            body,
            grid_spec=pltpu.PrefetchScalarGridSpec(
                num_scalar_prefetch=1,
                grid=grid,
                in_specs=list(in_specs) + [anywhere] * len(tokens),
                out_specs=out_specs,
                scratch_shapes=list(scratch),
            ),
            out_shape=out_shape,
            input_output_aliases=aliases or {},
            compiler_params=pltpu.CompilerParams(vmem_limit_bytes=limit),
            cost_estimate=pl.CostEstimate(flops=flops, bytes_accessed=2 * moved, transcendentals=0),
            name=name,
        )(self.at, *args, *tokens)
        if not free:
            self.last = [min(outs, key=lambda x: x.size)]
        return outs


def whole(shape):
    return pl.BlockSpec(shape, lambda i, at: (0,) * len(shape))


def like(pieces):
    return [whole(piece.shape) for piece in pieces]


def cut(chain, fields, which, across_px, across_py):
    layers, xb, yb = fields.shape[1:]
    groups = layers // across_py
    members = across_px // groups
    part = yb // members
    many = len(which)
    shape = (across_py, groups, members, many, xb, part)

    def copying(at, fields_ref, out, held, arrived, left):
        loads = [
            [
                pltpu.make_async_copy(
                    fields_ref.at[f, pl.ds(y * groups, groups), :, pl.ds(k * part, part)],
                    held.at[y, :, k, n],
                    arrived.at[y, k, n],
                )
                for k in range(members)
                for n, f in enumerate(which)
            ]
            for y in range(across_py)
        ]
        stores = [
            pltpu.make_async_copy(held.at[y], out.at[y], left.at[y]) for y in range(across_py)
        ]
        for block in loads:
            for copy in block:
                copy.start()
        for block, store in zip(loads, stores):
            for copy in block:
                copy.wait()
            store.start()
        for store in stores:
            store.wait()

    def slicing(at, *refs):
        for n in range(many):
            for k in range(members):
                refs[-1][0, :, k, n] = refs[n][0, :, :, k * part : (k + 1) * part]

    def field(f):
        return pl.BlockSpec((1, groups, xb, yb), lambda i, at: (f, i, 0, 0))

    if in_order(part):
        out = chain.run(
            "cut",
            copying,
            [fields],
            [anywhere],
            [anywhere],
            [jax.ShapeDtypeStruct(shape, fields.dtype)],
            scratch=[
                pltpu.VMEM(shape, fields.dtype),
                pltpu.SemaphoreType.DMA((across_py, members, many)),
                pltpu.SemaphoreType.DMA((across_py,)),
            ],
        )[0]
    else:
        out = chain.run(
            "cut",
            slicing,
            [fields] * many,
            [field(f) for f in which],
            [pl.BlockSpec((1,) + shape[1:], lambda i, at: (i, 0, 0, 0, 0, 0))],
            [jax.ShapeDtypeStruct(shape, fields.dtype)],
            grid=(across_py,),
            limit=SMALL_VMEM_BYTES,
        )[0]
    return out.reshape((across_py, across_px) + shape[3:])


def x_pass(chain, which, operators, viscosity, arrived, at_fields, members, speed):
    across_py, across_px, held, xb, part = arrived.shape
    fields = len(which)
    width = across_py * part
    length = across_px * xb
    rows = xb // members
    many = min(across_px, max(1, 256 // rows))
    steps = across_px // many
    first = speed is None
    only = fields == 1

    def kernel(at, visc_ref, op_ref, arrived_ref, *refs):
        speed_ref, outs, lines = refs[0], refs[1:-1], refs[-1]
        if first:
            speed_ref, outs = refs[-2], refs[:-2]
        step = pl.program_id(0)
        turn, place = step // steps, step % steps

        @pl.when(step == 0)
        def _():
            for x in range(across_px):
                rows_of = slice(x * xb, (x + 1) * xb)
                for y in range(across_py):
                    for n, field in enumerate(which):
                        start = n * width + y * part
                        piece = arrived_ref[y, x, 0 if only else at_fields.index(field)]
                        lines[rows_of, start : start + part] = piece
                    if first:
                        piece = arrived_ref[y, x, at_fields.index(U)]
                        speed_ref[rows_of, y * part : (y + 1) * part] = piece

        block = op_ref[...].reshape(3 * many * rows, length)
        whole_result = jnp.dot(block, lines[...], preferred_element_type=jnp.float32)
        for n, field in enumerate(which):
            result = whole_result[:, n * width : (n + 1) * width].reshape(3, many, rows, width)
            for c in range(many):
                if first:
                    row = (place * many + c) * xb + (at[1] ^ turn) * rows
                    u = speed_ref[pl.ds(pl.multiple_of(row, rows), rows), :]
                else:
                    u = speed_ref[c, 0]
                value = result[2, c] + time_step * (
                    -u.astype(jnp.float32) * result[0, c] + visc_ref[field] * result[1, c]
                )
                value = value.astype(jnp.bfloat16)
                for r in range(members):

                    @pl.when(turn == r)
                    def _():
                        outs[n * members + r][c] = value

    def out_block(r):
        return pl.BlockSpec(
            (many, rows, width), lambda i, at: (jnp.clip(i - r * steps, 0, steps - 1), 0, 0)
        )

    def place_of(i, at):
        return i % steps, at[1] ^ (i // steps), 0, 0

    in_specs = [
        smem,
        pl.BlockSpec((3, many, 1, rows, length), lambda i, at: (0,) + place_of(i, at)),
        pl.BlockSpec(
            (across_py, across_px, 1 if only else held, xb, part),
            lambda i, at: (0, 0, at_fields.index(which[0]) if only else 0, 0, 0),
        ),
    ]
    args = [viscosity, operators.reshape(3, across_px, members, rows, length), arrived]
    out_specs = [out_block(r) for _ in which for r in range(members)]
    out_shape = [jax.ShapeDtypeStruct((across_px, rows, width), jnp.bfloat16)] * len(out_specs)
    if first:
        out_specs.append(whole((length, width)))
        out_shape.append(jax.ShapeDtypeStruct((length, width), jnp.bfloat16))
    else:
        in_specs.append(pl.BlockSpec((many, 1, rows, width), place_of))
        args.append(speed.reshape(across_px, members, rows, width))
    outs = chain.run(
        "x_pass",
        kernel,
        args,
        in_specs,
        out_specs,
        out_shape,
        grid=(steps * members,),
        scratch=[pltpu.VMEM((length, fields * width), jnp.bfloat16)],
        flops=6 * length * length * width * fields,
        limit=MOST_VMEM_BYTES,
    )
    return [outs[n * members : (n + 1) * members] for n in range(fields)], outs[-1] if first else speed


def y_pass(chain, which, operators, viscosity, parts, speed, yb, shape):
    across_px, rows, width = parts[0][0].shape
    fields, members = len(parts), len(parts[0])
    part = yb // members
    length = width * members
    blocks = length // yb
    height = across_px * rows
    first = which[0] == V

    def kernel(at, visc_ref, op_ref, *refs):
        part_refs, rest = refs[: fields * members], refs[fields * members :]
        if first:
            out, speed_ref, lines = rest
        else:
            speed_ref, out, lines = rest
        step = pl.program_id(0)

        @pl.when(step == 0)
        def _():
            for n in range(fields):
                for r in range(members):
                    values = part_refs[n * members + r][...].reshape(height, width)
                    if in_order(part):
                        for y in range(blocks):
                            start = pl.multiple_of(y * yb + (at[1] ^ r) * part, part)
                            lines[n, :, pl.ds(start, part)] = values[:, y * part : (y + 1) * part]
                    else:
                        start = pl.multiple_of((at[1] ^ r) * width, width)
                        lines[n, :, pl.ds(start, width)] = values
            if first:
                for y in range(blocks):
                    if in_order(part):
                        speed_ref[y] = lines[0, :, y * yb : (y + 1) * yb]
                    else:
                        for k in range(members):
                            start = k * width + y * part
                            speed_ref[y, :, k * part : (k + 1) * part] = lines[0, :, start : start + part]

        v = speed_ref[step if first else 0].astype(jnp.float32)
        whole_result = lax.dot_general(
            lines[...].reshape(fields * height, length),
            op_ref[...].reshape(3 * yb, length),
            (((1,), (1,)), ((), ())),
            preferred_element_type=jnp.float32,
        )
        for n, field in enumerate(which):
            result = whole_result[n * height : (n + 1) * height]
            value = result[:, 2 * yb :] + time_step * (
                -v * result[:, :yb] + visc_ref[field] * result[:, yb : 2 * yb]
            )
            value = value.astype(jnp.bfloat16)
            out[0, :, n] = value.reshape(across_px, rows, yb)

    flat = [part for field_parts in parts for part in field_parts]
    in_specs = [smem, pl.BlockSpec((3, yb, length), lambda i, at: (0, i, 0))] + like(flat)
    args = [viscosity, operators, *flat]
    out_specs = [pl.BlockSpec((1,) + shape[1:], lambda i, at: (i, 0, 0, 0, 0))]
    out_shape = [jax.ShapeDtypeStruct(shape, jnp.bfloat16)]
    if first:
        out_specs.append(whole((blocks, height, yb)))
        out_shape.append(jax.ShapeDtypeStruct((blocks, height, yb), jnp.bfloat16))
    else:
        in_specs.append(pl.BlockSpec((1, height, yb), lambda i, at: (i, 0, 0)))
        args.append(speed)
    outs = chain.run(
        "y_pass",
        kernel,
        args,
        in_specs,
        out_specs,
        out_shape,
        grid=(blocks,),
        scratch=[pltpu.VMEM((fields, height, length), jnp.bfloat16)],
        flops=6 * length * length * height * fields,
        limit=MOST_VMEM_BYTES,
    )
    return outs[0], outs[1] if first else speed


def put(chain, buffer, arrived, which, block, shape):
    across_py, across_px = arrived.shape[:2]
    extra = [] if buffer is None else [buffer]
    many = len(which)
    first, stride = which[0], which[1] - which[0] if many > 1 else 0

    def kernel(at, arrived_ref, *refs):
        refs[-1][...] = arrived_ref[...].reshape(refs[-1].shape)

    return chain.run(
        "put",
        kernel,
        [arrived, *extra],
        [pl.BlockSpec((across_py, across_px, block) + arrived.shape[3:], lambda n, at: (0, 0, n, 0, 0))]
        + [anywhere] * len(extra),
        [pl.BlockSpec((1,) + shape[1:], lambda n, at: (first + n * stride, 0, 0, 0))],
        [jax.ShapeDtypeStruct(shape, arrived.dtype)],
        grid=(many,),
        aliases={2: 0} if extra else {},
        limit=SMALL_VMEM_BYTES,
        free=True,
    )[0]


def wall_lines(chain, arrived, n, tile, slot, unit):
    across_py, across_px, _, rows, yb = arrived.shape
    count, span = tile.shape[0], across_px * across_py * rows
    slots = across_py * across_px * unit

    def kernel(at, tile_ref, slot_ref, arrived_ref, *refs):
        outs, lines = refs[:-1], refs[-1]
        chosen = tile_ref[...] == lax.broadcasted_iota(jnp.int32, (count, span), 1)
        flux = jnp.dot(
            chosen.astype(jnp.float32).astype(jnp.bfloat16),
            arrived_ref[...].reshape(span, yb),
            preferred_element_type=jnp.float32,
        )
        filled = slot_ref[...] == lax.broadcasted_iota(jnp.int32, (slots, count), 0)
        lines[...] = jnp.dot(
            filled.astype(jnp.float32).astype(jnp.bfloat16),
            flux.astype(jnp.bfloat16),
            preferred_element_type=jnp.float32,
        ).reshape(lines.shape)
        for s in range(across_py):
            outs[s][...] = lines[at[2] ^ s].astype(jnp.bfloat16)

    args = [tile.reshape(-1, 1), slot.reshape(1, -1)]
    shape = (across_px, unit, yb)
    return chain.run(
        "wall_lines",
        kernel,
        args + [arrived],
        like(args)
        + [pl.BlockSpec((across_py, across_px, 1, rows, yb), lambda i, at: (0, 0, n, 0, 0))],
        [whole(shape)] * across_py,
        [jax.ShapeDtypeStruct(shape, jnp.bfloat16)] * across_py,
        scratch=[pltpu.VMEM((across_py,) + shape, jnp.float32)],
        limit=SMALL_VMEM_BYTES,
    )


def wall_columns(chain, pieces):
    across_py, (across_px, unit, yb) = len(pieces), pieces[0].shape

    def kernel(at, *refs):
        outs = refs[across_py:]
        for t in range(across_px):
            for s in range(across_py):
                outs[t][at[2] ^ s] = refs[s][at[7] ^ t]

    shape = (across_py, unit, yb)
    return chain.run(
        "wall_columns",
        kernel,
        [*pieces],
        like(pieces),
        [whole(shape)] * across_px,
        [jax.ShapeDtypeStruct(shape, jnp.bfloat16)] * across_px,
        limit=SMALL_VMEM_BYTES,
    )


def add_flux(chain, tags, arrived, solid_temp, conductivity):
    rows, columns = solid_temp.shape
    across_px, (across_py, unit, _) = len(arrived), arrived[0].shape

    def kernel(at, temp_ref, kappa_ref, *refs):
        line_refs, tag_refs, out = refs[:across_px], refs[across_px:-1], refs[-1]
        out[0] = temp_ref[...]
        out[1] = kappa_ref[...]
        places = lax.broadcasted_iota(jnp.int32, (rows, unit), 0)
        source = jnp.zeros((rows, columns), jnp.float32)
        for s in range(across_py):
            chosen = [(tag_refs[s][t] == places).astype(jnp.float32) for t in range(across_px)]
            lines = [line_refs[t][at[2] ^ s] for t in range(across_px)]
            source = source + jnp.dot(
                jnp.concatenate(chosen, axis=1).astype(jnp.bfloat16),
                jnp.concatenate(lines, axis=0),
                preferred_element_type=jnp.float32,
            )
        out[2] = (wall_gain * source_gain) * source

    args = [solid_temp, conductivity, *arrived, *tags]
    return chain.run(
        "add_flux",
        kernel,
        args,
        like(args),
        [whole((3, rows, columns))],
        [jax.ShapeDtypeStruct((3, rows, columns), jnp.float32)],
        limit=SMALL_VMEM_BYTES,
    )[0]


def conduct(chain, solid, low, high, margin):
    kinds, height, columns = solid.shape
    rows = height - 2 * margin
    wide = columns + -(-2 * margin // 128) * 128

    def kernel(at, solid_ref, low_ref, high_ref, out, ext):
        ext[:, :, columns:] = jnp.zeros((kinds, height, wide - columns), jnp.float32)
        ext[:, :, :columns] = solid_ref[...]
        ext[:, :, columns : columns + margin] = high_ref[...]
        ext[:, :, wide - margin :] = low_ref[...]
        t, kappa, heat = ext[0], ext[1], ext[2]
        row = lax.broadcasted_iota(jnp.int32, (height, wide), 0) + at[3]
        col = lax.broadcasted_iota(jnp.int32, (height, wide), 1)
        col = jnp.where(col < wide - margin, col, col - wide) + at[4]
        inside = (row >= 0) & (row < at[5]) & (col >= 0) & (col < at[6])
        moves = ((height - 1, 0), (1, 0), (wide - 1, 1), (1, 1))
        faces = [
            jnp.where(inside, diffusion_rate * 0.5 * (kappa + pltpu.roll(kappa, shift, dim)), 0.0)
            for shift, dim in moves
        ]
        for _ in range(COND_STEPS):
            change = heat
            for face, (shift, dim) in zip(faces, moves):
                change = change + face * (pltpu.roll(t, shift, dim) - t)
            t = t + change
        out[...] = t[margin : margin + rows, :columns]

    args = [solid, low, high]
    return chain.run(
        "conduct",
        kernel,
        args,
        like(args),
        [whole((rows, columns))],
        [jax.ShapeDtypeStruct((rows, columns), jnp.float32)],
        scratch=[pltpu.VMEM((kinds, height, wide), jnp.float32)],
        limit=SMALL_VMEM_BYTES,
    )[0]


def on_device(
    fields,
    x_operators,
    y_operators,
    viscosity,
    wall_tile,
    wall_owner,
    wall_row,
    solid_temp,
    conductivity,
):
    across_px, across_py = lax.axis_size("px"), lax.axis_size("py")
    devices = across_px * across_py
    layers, xb, yb = fields.shape[1:]
    groups = layers // across_py
    members = across_px // groups
    a, b = lax.axis_index("px"), lax.axis_index("py")
    q, m = a // members, a % members
    rows, columns = solid_temp.shape
    margin = COND_STEPS
    at = jnp.stack(
        [
            q,
            m,
            b,
            a * rows - margin,
            b * columns,
            across_px * rows,
            across_py * columns,
            a,
        ]
    ).astype(jnp.int32)
    chain = Chain(at)

    def along(axis, pieces):
        return [pieces[0]] + [
            lax.ppermute(piece, axis, [(i, i ^ s) for i in range(lax.axis_size(axis))])
            for s, piece in enumerate(pieces[1:], 1)
        ]

    def exchange(blocks):
        moved = lax.all_to_all(
            blocks.reshape((devices,) + blocks.shape[2:]),
            ("py", "px"),
            split_axis=0,
            concat_axis=0,
            tiled=True,
        )
        return moved.reshape(blocks.shape)

    half, speeds = {}, {}

    def forward(*which):
        return exchange(cut(chain, fields, which, across_px, across_py))

    def X(arrived, at_fields, *which):
        outs, speeds[U] = x_pass(
            chain, which, x_operators, viscosity, arrived, at_fields, members, speeds.get(U)
        )
        for f, out in zip(which, outs):
            half[f] = along("px", out)

    y_columns = y_operators
    if not in_order(yb // members):
        y_columns = y_columns.reshape(3, -1, across_py, members, yb // members)
        y_columns = y_columns.swapaxes(2, 3).reshape(y_operators.shape)

    def Y(*which):
        shape = (across_py, across_px, len(which), xb // members, yb)
        out, speeds[V] = y_pass(
            chain,
            which,
            y_columns,
            viscosity,
            [half[f] for f in which],
            speeds.get(V),
            yb,
            shape,
        )
        return out

    most = forward(U, V, THETA)

    count = wall_tile.shape[0]
    owner = wall_owner[:, 0]
    unit = max(2, 4 * count // devices)
    order = jnp.arange(count, dtype=jnp.int32)
    earlier = (owner[:, None] == owner[None, :]) & (order[None, :] < order[:, None])
    position = jnp.sum(earlier.astype(jnp.int32), axis=1)
    label = owner * unit + position
    filled = label[None, :] == jnp.arange(devices * unit, dtype=jnp.int32)[:, None]
    labels = jnp.sum(jnp.where(filled, wall_row[None, :] + 1, 0), axis=1) - 1
    labels = labels.reshape(across_px, across_py, unit)
    slot = (owner % across_py * across_px + owner // across_py) * unit + position
    tags = along(
        "px",
        [lax.dynamic_index_in_dim(labels, a ^ s, 0, keepdims=False) for s in range(across_px)],
    )
    chain.last += tags
    last = forward(W)
    tags = along(
        "py",
        [
            jnp.stack([lax.dynamic_index_in_dim(tag, b ^ s, 0) for tag in tags])
            for s in range(across_py)
        ],
    )

    X(most, (U, V, THETA), V, THETA)
    first = exchange(Y(V, THETA))
    X(most, (U, V, THETA), U)
    X(last, (W,), W)
    second = Y(U, W)
    chain.last += tags
    flux = along("py", wall_lines(chain, first, 1, wall_tile, slot, unit))
    flux, second = lax.optimization_barrier((wall_columns(chain, flux), second))
    second = exchange(second)
    solid = add_flux(chain, tags, along("px", flux), solid_temp, conductivity)
    new_fields = put(chain, None, first, (V, THETA), 1, fields.shape)
    low, high = margins(solid, "px", 1, margin)
    solid = jnp.concatenate([low, solid, high], axis=1)
    low, high = margins(solid, "py", 2, margin)
    new_solid = conduct(chain, solid, low, high, margin)
    new_fields = put(chain, new_fields, second, (U, W), 1, fields.shape)
    return new_fields, new_solid


def solution(mesh):
    return jax.shard_map(
        on_device,
        mesh=mesh,
        in_specs=(
            P(None, None, "px", "py"),
            P(),
            P(),
            P(),
            P(("px", "py")),
            P(("px", "py"), None),
            P(("px", "py")),
            P("px", "py"),
            P("px", "py"),
        ),
        out_specs=(P(None, None, "px", "py"), P("px", "py")),
        check_vma=False,
    )
```

```python
import jax
import jax.numpy as jnp
from jax import lax
from jax.experimental import pallas as pl
from jax.experimental.pallas import tpu as pltpu
from jax.sharding import PartitionSpec as P

COND_STEPS = 8

time_step = 0.25
wall_gain = 0.5
diffusion_rate = 0.24
source_gain = 0.1

U, V, W, THETA = 0, 1, 2, 3
SMALL_VMEM_BYTES = 16 * 1024 * 1024
MOST_VMEM_BYTES = 56 * 1024 * 1024

smem = pl.BlockSpec(memory_space=pltpu.SMEM)
anywhere = pl.BlockSpec(memory_space=pl.ANY)


def margins(block, axis, dim, width):
    count = lax.axis_size(axis)
    forward = [(i, i + 1) for i in range(count - 1)]
    backward = [(target, source) for source, target in forward]
    low = lax.ppermute(
        lax.slice_in_dim(block, block.shape[dim] - width, None, axis=dim), axis, forward
    )
    high = lax.ppermute(lax.slice_in_dim(block, 0, width, axis=dim), axis, backward)
    return low, high


def in_order(part):
    return part % 128 == 0


class Chain:
    def __init__(self, at):
        self.at = at
        self.last = []

    def run(
        self,
        name,
        kernel,
        args,
        in_specs,
        out_specs,
        out_shape,
        grid=(1,),
        scratch=(),
        aliases=None,
        flops=0,
        limit=MOST_VMEM_BYTES,
        free=False,
    ):
        count = len(args)
        tokens = [] if free else [x for x in self.last if not any(x is y for y in args)]

        def body(at_ref, *refs):
            kernel(at_ref, *refs[:count], *refs[count + len(tokens) :])

        moved = sum(x.size * x.dtype.itemsize for x in out_shape)
        outs = pl.pallas_call(
            body,
            grid_spec=pltpu.PrefetchScalarGridSpec(
                num_scalar_prefetch=1,
                grid=grid,
                in_specs=list(in_specs) + [anywhere] * len(tokens),
                out_specs=out_specs,
                scratch_shapes=list(scratch),
            ),
            out_shape=out_shape,
            input_output_aliases=aliases or {},
            compiler_params=pltpu.CompilerParams(vmem_limit_bytes=limit),
            cost_estimate=pl.CostEstimate(flops=flops, bytes_accessed=2 * moved, transcendentals=0),
            name=name,
        )(self.at, *args, *tokens)
        if not free:
            self.last = [min(outs, key=lambda x: x.size)]
        return outs


def whole(shape):
    return pl.BlockSpec(shape, lambda i, at: (0,) * len(shape))


def like(pieces):
    return [whole(piece.shape) for piece in pieces]


def cut(chain, fields, which, across_px, across_py):
    layers, xb, yb = fields.shape[1:]
    groups = layers // across_py
    members = across_px // groups
    part = yb // members
    many = len(which)
    shape = (across_py, groups, members, many, xb, part)

    def copying(at, fields_ref, out, held, arrived, left):
        loads = [
            [
                pltpu.make_async_copy(
                    fields_ref.at[f, pl.ds(y * groups, groups), :, pl.ds(k * part, part)],
                    held.at[y, :, k, n],
                    arrived.at[y, k, n],
                )
                for k in range(members)
                for n, f in enumerate(which)
            ]
            for y in range(across_py)
        ]
        stores = [
            pltpu.make_async_copy(held.at[y], out.at[y], left.at[y]) for y in range(across_py)
        ]
        for block in loads:
            for copy in block:
                copy.start()
        for block, store in zip(loads, stores):
            for copy in block:
                copy.wait()
            store.start()
        for store in stores:
            store.wait()

    def slicing(at, *refs):
        for n in range(many):
            for k in range(members):
                refs[-1][0, :, k, n] = refs[n][0, :, :, k * part : (k + 1) * part]

    def field(f):
        return pl.BlockSpec((1, groups, xb, yb), lambda i, at: (f, i, 0, 0))

    if in_order(part):
        out = chain.run(
            "cut",
            copying,
            [fields],
            [anywhere],
            [anywhere],
            [jax.ShapeDtypeStruct(shape, fields.dtype)],
            scratch=[
                pltpu.VMEM(shape, fields.dtype),
                pltpu.SemaphoreType.DMA((across_py, members, many)),
                pltpu.SemaphoreType.DMA((across_py,)),
            ],
        )[0]
    else:
        out = chain.run(
            "cut",
            slicing,
            [fields] * many,
            [field(f) for f in which],
            [pl.BlockSpec((1,) + shape[1:], lambda i, at: (i, 0, 0, 0, 0, 0))],
            [jax.ShapeDtypeStruct(shape, fields.dtype)],
            grid=(across_py,),
            limit=SMALL_VMEM_BYTES,
        )[0]
    return out.reshape((across_py, across_px) + shape[3:])


def x_pass(chain, which, operators, viscosity, arrived, at_fields, members, speed):
    across_py, across_px, held, xb, part = arrived.shape
    fields = len(which)
    width = across_py * part
    length = across_px * xb
    rows = xb // members
    many = min(across_px, max(1, 256 // rows))
    steps = across_px // many
    first = speed is None
    only = fields == 1

    def kernel(at, visc_ref, op_ref, arrived_ref, *refs):
        speed_ref, outs, lines = refs[0], refs[1:-1], refs[-1]
        if first:
            speed_ref, outs = refs[-2], refs[:-2]
        step = pl.program_id(0)
        turn, place = step // steps, step % steps

        @pl.when(step == 0)
        def _():
            for x in range(across_px):
                rows_of = slice(x * xb, (x + 1) * xb)
                for y in range(across_py):
                    for n, field in enumerate(which):
                        start = n * width + y * part
                        piece = arrived_ref[y, x, 0 if only else at_fields.index(field)]
                        lines[rows_of, start : start + part] = piece
                    if first:
                        piece = arrived_ref[y, x, at_fields.index(U)]
                        speed_ref[rows_of, y * part : (y + 1) * part] = piece

        block = op_ref[...].reshape(3 * many * rows, length)
        whole_result = jnp.dot(block, lines[...], preferred_element_type=jnp.float32)
        for n, field in enumerate(which):
            result = whole_result[:, n * width : (n + 1) * width].reshape(3, many, rows, width)
            for c in range(many):
                if first:
                    row = (place * many + c) * xb + (at[1] ^ turn) * rows
                    u = speed_ref[pl.ds(pl.multiple_of(row, rows), rows), :]
                else:
                    u = speed_ref[c, 0]
                value = result[2, c] + time_step * (
                    -u.astype(jnp.float32) * result[0, c] + visc_ref[field] * result[1, c]
                )
                value = value.astype(jnp.bfloat16)
                for r in range(members):

                    @pl.when(turn == r)
                    def _():
                        outs[n * members + r][c] = value

    def out_block(r):
        return pl.BlockSpec(
            (many, rows, width), lambda i, at: (jnp.clip(i - r * steps, 0, steps - 1), 0, 0)
        )

    def place_of(i, at):
        return i % steps, at[1] ^ (i // steps), 0, 0

    in_specs = [
        smem,
        pl.BlockSpec((3, many, 1, rows, length), lambda i, at: (0,) + place_of(i, at)),
        pl.BlockSpec(
            (across_py, across_px, 1 if only else held, xb, part),
            lambda i, at: (0, 0, at_fields.index(which[0]) if only else 0, 0, 0),
        ),
    ]
    args = [viscosity, operators.reshape(3, across_px, members, rows, length), arrived]
    out_specs = [out_block(r) for _ in which for r in range(members)]
    out_shape = [jax.ShapeDtypeStruct((across_px, rows, width), jnp.bfloat16)] * len(out_specs)
    if first:
        out_specs.append(whole((length, width)))
        out_shape.append(jax.ShapeDtypeStruct((length, width), jnp.bfloat16))
    else:
        in_specs.append(pl.BlockSpec((many, 1, rows, width), place_of))
        args.append(speed.reshape(across_px, members, rows, width))
    outs = chain.run(
        "x_pass",
        kernel,
        args,
        in_specs,
        out_specs,
        out_shape,
        grid=(steps * members,),
        scratch=[pltpu.VMEM((length, fields * width), jnp.bfloat16)],
        flops=6 * length * length * width * fields,
        limit=MOST_VMEM_BYTES,
    )
    return [outs[n * members : (n + 1) * members] for n in range(fields)], outs[-1] if first else speed


def y_pass(chain, which, operators, viscosity, parts, speed, yb, shape):
    across_px, rows, width = parts[0][0].shape
    fields, members = len(parts), len(parts[0])
    part = yb // members
    length = width * members
    blocks = length // yb
    height = across_px * rows
    first = which[0] == V

    def kernel(at, visc_ref, op_ref, *refs):
        part_refs, rest = refs[: fields * members], refs[fields * members :]
        if first:
            out, speed_ref, lines = rest
        else:
            speed_ref, out, mark, lines = rest
            mark[...] = jnp.zeros_like(mark)
        step = pl.program_id(0)

        @pl.when(step == 0)
        def _():
            for n in range(fields):
                for r in range(members):
                    values = part_refs[n * members + r][...].reshape(height, width)
                    if in_order(part):
                        for y in range(blocks):
                            start = pl.multiple_of(y * yb + (at[1] ^ r) * part, part)
                            lines[n, :, pl.ds(start, part)] = values[:, y * part : (y + 1) * part]
                    else:
                        start = pl.multiple_of((at[1] ^ r) * width, width)
                        lines[n, :, pl.ds(start, width)] = values
            if first:
                for y in range(blocks):
                    if in_order(part):
                        speed_ref[y] = lines[0, :, y * yb : (y + 1) * yb]
                    else:
                        for k in range(members):
                            start = k * width + y * part
                            speed_ref[y, :, k * part : (k + 1) * part] = lines[0, :, start : start + part]

        v = speed_ref[step if first else 0].astype(jnp.float32)
        whole_result = lax.dot_general(
            lines[...].reshape(fields * height, length),
            op_ref[...].reshape(3 * yb, length),
            (((1,), (1,)), ((), ())),
            preferred_element_type=jnp.float32,
        )
        for n, field in enumerate(which):
            result = whole_result[n * height : (n + 1) * height]
            value = result[:, 2 * yb :] + time_step * (
                -v * result[:, :yb] + visc_ref[field] * result[:, yb : 2 * yb]
            )
            value = value.astype(jnp.bfloat16)
            out[0, :, n] = value.reshape(across_px, rows, yb)

    flat = [part for field_parts in parts for part in field_parts]
    in_specs = [smem, pl.BlockSpec((3, yb, length), lambda i, at: (0, i, 0))] + like(flat)
    args = [viscosity, operators, *flat]
    out_specs = [pl.BlockSpec((1,) + shape[1:], lambda i, at: (i, 0, 0, 0, 0))]
    out_shape = [jax.ShapeDtypeStruct(shape, jnp.bfloat16)]
    if first:
        out_specs.append(whole((blocks, height, yb)))
        out_shape.append(jax.ShapeDtypeStruct((blocks, height, yb), jnp.bfloat16))
    else:
        in_specs.append(pl.BlockSpec((1, height, yb), lambda i, at: (i, 0, 0)))
        args.append(speed)
        out_specs.append(whole((8, 128)))
        out_shape.append(jax.ShapeDtypeStruct((8, 128), jnp.float32))
    outs = chain.run(
        "y_pass",
        kernel,
        args,
        in_specs,
        out_specs,
        out_shape,
        grid=(blocks,),
        scratch=[pltpu.VMEM((fields, height, length), jnp.bfloat16)],
        flops=6 * length * length * height * fields,
        limit=MOST_VMEM_BYTES,
    )
    return outs[0], outs[1] if first else speed


def put(chain, buffer, arrived, which, block, shape):
    across_py, across_px = arrived.shape[:2]
    extra = [] if buffer is None else [buffer]
    many = len(which)
    first, stride = which[0], which[1] - which[0] if many > 1 else 0

    def kernel(at, arrived_ref, *refs):
        refs[-1][...] = arrived_ref[...].reshape(refs[-1].shape)

    return chain.run(
        "put",
        kernel,
        [arrived, *extra],
        [pl.BlockSpec((across_py, across_px, block) + arrived.shape[3:], lambda n, at: (0, 0, n, 0, 0))]
        + [anywhere] * len(extra),
        [pl.BlockSpec((1,) + shape[1:], lambda n, at: (first + n * stride, 0, 0, 0))],
        [jax.ShapeDtypeStruct(shape, arrived.dtype)],
        grid=(many,),
        aliases={2: 0} if extra else {},
        limit=SMALL_VMEM_BYTES,
        free=True,
    )[0]


def wall_lines(chain, arrived, n, tile, slot, unit):
    across_py, across_px, _, rows, yb = arrived.shape
    count, span = tile.shape[0], across_px * across_py * rows
    slots = across_py * across_px * unit

    def kernel(at, tile_ref, slot_ref, arrived_ref, *refs):
        outs, lines = refs[:-1], refs[-1]
        chosen = tile_ref[...] == lax.broadcasted_iota(jnp.int32, (count, span), 1)
        flux = jnp.dot(
            chosen.astype(jnp.float32).astype(jnp.bfloat16),
            arrived_ref[...].reshape(span, yb),
            preferred_element_type=jnp.float32,
        )
        filled = slot_ref[...] == lax.broadcasted_iota(jnp.int32, (slots, count), 0)
        lines[...] = jnp.dot(
            filled.astype(jnp.float32).astype(jnp.bfloat16),
            flux.astype(jnp.bfloat16),
            preferred_element_type=jnp.float32,
        ).reshape(lines.shape)
        for s in range(across_py):
            outs[s][...] = lines[at[2] ^ s].astype(jnp.bfloat16)

    args = [tile.reshape(-1, 1), slot.reshape(1, -1)]
    shape = (across_px, unit, yb)
    return chain.run(
        "wall_lines",
        kernel,
        args + [arrived],
        like(args)
        + [pl.BlockSpec((across_py, across_px, 1, rows, yb), lambda i, at: (0, 0, n, 0, 0))],
        [whole(shape)] * across_py,
        [jax.ShapeDtypeStruct(shape, jnp.bfloat16)] * across_py,
        scratch=[pltpu.VMEM((across_py,) + shape, jnp.float32)],
        limit=SMALL_VMEM_BYTES,
    )


def wall_columns(chain, pieces):
    across_py, (across_px, unit, yb) = len(pieces), pieces[0].shape

    def kernel(at, *refs):
        outs = refs[across_py:]
        for t in range(across_px):
            for s in range(across_py):
                outs[t][at[2] ^ s] = refs[s][at[7] ^ t]

    shape = (across_py, unit, yb)
    return chain.run(
        "wall_columns",
        kernel,
        [*pieces],
        like(pieces),
        [whole(shape)] * across_px,
        [jax.ShapeDtypeStruct(shape, jnp.bfloat16)] * across_px,
        limit=SMALL_VMEM_BYTES,
    )


def add_flux(chain, tags, arrived, solid_temp, conductivity):
    rows, columns = solid_temp.shape
    across_px, (across_py, unit, _) = len(arrived), arrived[0].shape

    def kernel(at, temp_ref, kappa_ref, *refs):
        line_refs, tag_refs, out = refs[:across_px], refs[across_px:-1], refs[-1]
        out[0] = temp_ref[...]
        out[1] = kappa_ref[...]
        places = lax.broadcasted_iota(jnp.int32, (rows, unit), 0)
        source = jnp.zeros((rows, columns), jnp.float32)
        for s in range(across_py):
            chosen = [(tag_refs[s][t] == places).astype(jnp.float32) for t in range(across_px)]
            lines = [line_refs[t][at[2] ^ s] for t in range(across_px)]
            source = source + jnp.dot(
                jnp.concatenate(chosen, axis=1).astype(jnp.bfloat16),
                jnp.concatenate(lines, axis=0),
                preferred_element_type=jnp.float32,
            )
        out[2] = (wall_gain * source_gain) * source

    args = [solid_temp, conductivity, *arrived, *tags]
    return chain.run(
        "add_flux",
        kernel,
        args,
        like(args),
        [whole((3, rows, columns))],
        [jax.ShapeDtypeStruct((3, rows, columns), jnp.float32)],
        limit=SMALL_VMEM_BYTES,
    )[0]


def conduct(chain, solid, low, high, margin):
    kinds, height, columns = solid.shape
    rows = height - 2 * margin
    wide = columns + -(-2 * margin // 128) * 128

    def kernel(at, solid_ref, low_ref, high_ref, out, ext):
        ext[:, :, columns:] = jnp.zeros((kinds, height, wide - columns), jnp.float32)
        ext[:, :, :columns] = solid_ref[...]
        ext[:, :, columns : columns + margin] = high_ref[...]
        ext[:, :, wide - margin :] = low_ref[...]
        t, kappa, heat = ext[0], ext[1], ext[2]
        row = lax.broadcasted_iota(jnp.int32, (height, wide), 0) + at[3]
        col = lax.broadcasted_iota(jnp.int32, (height, wide), 1)
        col = jnp.where(col < wide - margin, col, col - wide) + at[4]
        inside = (row >= 0) & (row < at[5]) & (col >= 0) & (col < at[6])
        moves = ((height - 1, 0), (1, 0), (wide - 1, 1), (1, 1))
        faces = [
            jnp.where(inside, diffusion_rate * 0.5 * (kappa + pltpu.roll(kappa, shift, dim)), 0.0)
            for shift, dim in moves
        ]
        for _ in range(COND_STEPS):
            change = heat
            for face, (shift, dim) in zip(faces, moves):
                change = change + face * (pltpu.roll(t, shift, dim) - t)
            t = t + change
        out[...] = t[margin : margin + rows, :columns]

    args = [solid, low, high]
    return chain.run(
        "conduct",
        kernel,
        args,
        like(args),
        [whole((rows, columns))],
        [jax.ShapeDtypeStruct((rows, columns), jnp.float32)],
        scratch=[pltpu.VMEM((kinds, height, wide), jnp.float32)],
        limit=SMALL_VMEM_BYTES,
    )[0]


def on_device(
    fields,
    x_operators,
    y_operators,
    viscosity,
    wall_tile,
    wall_owner,
    wall_row,
    solid_temp,
    conductivity,
):
    across_px, across_py = lax.axis_size("px"), lax.axis_size("py")
    devices = across_px * across_py
    layers, xb, yb = fields.shape[1:]
    groups = layers // across_py
    members = across_px // groups
    a, b = lax.axis_index("px"), lax.axis_index("py")
    q, m = a // members, a % members
    rows, columns = solid_temp.shape
    margin = COND_STEPS
    at = jnp.stack(
        [
            q,
            m,
            b,
            a * rows - margin,
            b * columns,
            across_px * rows,
            across_py * columns,
            a,
        ]
    ).astype(jnp.int32)
    chain = Chain(at)

    def along(axis, pieces):
        return [pieces[0]] + [
            lax.ppermute(piece, axis, [(i, i ^ s) for i in range(lax.axis_size(axis))])
            for s, piece in enumerate(pieces[1:], 1)
        ]

    def exchange(blocks):
        moved = lax.all_to_all(
            blocks.reshape((devices,) + blocks.shape[2:]),
            ("py", "px"),
            split_axis=0,
            concat_axis=0,
            tiled=True,
        )
        return moved.reshape(blocks.shape)

    half, speeds = {}, {}

    def forward(*which):
        return exchange(cut(chain, fields, which, across_px, across_py))

    def X(arrived, at_fields, *which):
        outs, speeds[U] = x_pass(
            chain, which, x_operators, viscosity, arrived, at_fields, members, speeds.get(U)
        )
        for f, out in zip(which, outs):
            half[f] = along("px", out)

    y_columns = y_operators
    if not in_order(yb // members):
        y_columns = y_columns.reshape(3, -1, across_py, members, yb // members)
        y_columns = y_columns.swapaxes(2, 3).reshape(y_operators.shape)

    def Y(*which):
        shape = (across_py, across_px, len(which), xb // members, yb)
        out, speeds[V] = y_pass(
            chain,
            which,
            y_columns,
            viscosity,
            [half[f] for f in which],
            speeds.get(V),
            yb,
            shape,
        )
        return out

    most = forward(U, V, THETA)

    count = wall_tile.shape[0]
    owner = wall_owner[:, 0]
    unit = max(2, 4 * count // devices)
    order = jnp.arange(count, dtype=jnp.int32)
    earlier = (owner[:, None] == owner[None, :]) & (order[None, :] < order[:, None])
    position = jnp.sum(earlier.astype(jnp.int32), axis=1)
    label = owner * unit + position
    filled = label[None, :] == jnp.arange(devices * unit, dtype=jnp.int32)[:, None]
    labels = jnp.sum(jnp.where(filled, wall_row[None, :] + 1, 0), axis=1) - 1
    labels = labels.reshape(across_px, across_py, unit)
    slot = (owner % across_py * across_px + owner // across_py) * unit + position
    tags = along(
        "px",
        [lax.dynamic_index_in_dim(labels, a ^ s, 0, keepdims=False) for s in range(across_px)],
    )
    chain.last += tags
    last = forward(W)
    tags = along(
        "py",
        [
            jnp.stack([lax.dynamic_index_in_dim(tag, b ^ s, 0) for tag in tags])
            for s in range(across_py)
        ],
    )

    X(most, (U, V, THETA), V, THETA)
    first = exchange(Y(V, THETA))
    X(most, (U, V, THETA), U)
    X(last, (W,), W)
    second = Y(U, W)
    chain.last += tags
    flux = along("py", wall_lines(chain, first, 1, wall_tile, slot, unit))
    flux, second = lax.optimization_barrier((flux, second))
    second = exchange(second)
    flux = wall_columns(chain, flux)
    solid = add_flux(chain, tags, along("px", flux), solid_temp, conductivity)
    new_fields = put(chain, None, first, (V, THETA), 1, fields.shape)
    low, high = margins(solid, "px", 1, margin)
    solid = jnp.concatenate([low, solid, high], axis=1)
    low, high = margins(solid, "py", 2, margin)
    new_solid = conduct(chain, solid, low, high, margin)
    new_fields = put(chain, new_fields, second, (U, W), 1, fields.shape)
    return new_fields, new_solid


def solution(mesh):
    return jax.shard_map(
        on_device,
        mesh=mesh,
        in_specs=(
            P(None, None, "px", "py"),
            P(),
            P(),
            P(),
            P(("px", "py")),
            P(("px", "py"), None),
            P(("px", "py")),
            P("px", "py"),
            P("px", "py"),
        ),
        out_specs=(P(None, None, "px", "py"), P("px", "py")),
        check_vma=False,
    )
```

```python
import jax
import jax.numpy as jnp
from jax import lax
from jax.experimental import pallas as pl
from jax.experimental.pallas import tpu as pltpu
from jax.sharding import PartitionSpec as P

COND_STEPS = 8

time_step = 0.25
wall_gain = 0.5
diffusion_rate = 0.24
source_gain = 0.1

U, V, W, THETA = 0, 1, 2, 3
SMALL_VMEM_BYTES = 16 * 1024 * 1024
MOST_VMEM_BYTES = 56 * 1024 * 1024

smem = pl.BlockSpec(memory_space=pltpu.SMEM)
anywhere = pl.BlockSpec(memory_space=pl.ANY)


def margins(block, axis, dim, width):
    count = lax.axis_size(axis)
    forward = [(i, i + 1) for i in range(count - 1)]
    backward = [(target, source) for source, target in forward]
    low = lax.ppermute(
        lax.slice_in_dim(block, block.shape[dim] - width, None, axis=dim), axis, forward
    )
    high = lax.ppermute(lax.slice_in_dim(block, 0, width, axis=dim), axis, backward)
    return low, high


def in_order(part):
    return part % 128 == 0


class Chain:
    def __init__(self, at):
        self.at = at
        self.last = []

    def run(
        self,
        name,
        kernel,
        args,
        in_specs,
        out_specs,
        out_shape,
        grid=(1,),
        scratch=(),
        aliases=None,
        flops=0,
        limit=MOST_VMEM_BYTES,
        free=False,
    ):
        count = len(args)
        tokens = [] if free else [x for x in self.last if not any(x is y for y in args)]

        def body(at_ref, *refs):
            kernel(at_ref, *refs[:count], *refs[count + len(tokens) :])

        moved = sum(x.size * x.dtype.itemsize for x in out_shape)
        outs = pl.pallas_call(
            body,
            grid_spec=pltpu.PrefetchScalarGridSpec(
                num_scalar_prefetch=1,
                grid=grid,
                in_specs=list(in_specs) + [anywhere] * len(tokens),
                out_specs=out_specs,
                scratch_shapes=list(scratch),
            ),
            out_shape=out_shape,
            input_output_aliases=aliases or {},
            compiler_params=pltpu.CompilerParams(vmem_limit_bytes=limit),
            cost_estimate=pl.CostEstimate(flops=flops, bytes_accessed=2 * moved, transcendentals=0),
            name=name,
        )(self.at, *args, *tokens)
        if not free:
            self.last = [min(outs, key=lambda x: x.size)]
        return outs


def whole(shape):
    return pl.BlockSpec(shape, lambda i, at: (0,) * len(shape))


def like(pieces):
    return [whole(piece.shape) for piece in pieces]


def cut(chain, fields, which, across_px, across_py):
    layers, xb, yb = fields.shape[1:]
    groups = layers // across_py
    members = across_px // groups
    part = yb // members
    many = len(which)
    shape = (across_py, groups, members, many, xb, part)

    def copying(at, fields_ref, out, held, arrived, left):
        loads = [
            [
                pltpu.make_async_copy(
                    fields_ref.at[f, pl.ds(y * groups, groups), :, pl.ds(k * part, part)],
                    held.at[y, :, k, n],
                    arrived.at[y, k, n],
                )
                for k in range(members)
                for n, f in enumerate(which)
            ]
            for y in range(across_py)
        ]
        stores = [
            pltpu.make_async_copy(held.at[y], out.at[y], left.at[y]) for y in range(across_py)
        ]
        for block in loads:
            for copy in block:
                copy.start()
        for block, store in zip(loads, stores):
            for copy in block:
                copy.wait()
            store.start()
        for store in stores:
            store.wait()

    def slicing(at, *refs):
        for n in range(many):
            for k in range(members):
                refs[-1][0, :, k, n] = refs[n][0, :, :, k * part : (k + 1) * part]

    def field(f):
        return pl.BlockSpec((1, groups, xb, yb), lambda i, at: (f, i, 0, 0))

    if in_order(part):
        out = chain.run(
            "cut",
            copying,
            [fields],
            [anywhere],
            [anywhere],
            [jax.ShapeDtypeStruct(shape, fields.dtype)],
            scratch=[
                pltpu.VMEM(shape, fields.dtype),
                pltpu.SemaphoreType.DMA((across_py, members, many)),
                pltpu.SemaphoreType.DMA((across_py,)),
            ],
        )[0]
    else:
        out = chain.run(
            "cut",
            slicing,
            [fields] * many,
            [field(f) for f in which],
            [pl.BlockSpec((1,) + shape[1:], lambda i, at: (i, 0, 0, 0, 0, 0))],
            [jax.ShapeDtypeStruct(shape, fields.dtype)],
            grid=(across_py,),
            limit=SMALL_VMEM_BYTES,
        )[0]
    return out.reshape((across_py, across_px) + shape[3:])


def x_pass(chain, which, operators, viscosity, arrived, at_fields, members, speed):
    across_py, across_px, held, xb, part = arrived.shape
    fields = len(which)
    width = across_py * part
    length = across_px * xb
    rows = xb // members
    many = min(across_px, max(1, 256 // rows))
    steps = across_px // many
    first = speed is None
    only = fields == 1

    def kernel(at, visc_ref, op_ref, arrived_ref, *refs):
        speed_ref, outs, lines = refs[0], refs[1:-1], refs[-1]
        if first:
            speed_ref, outs = refs[-2], refs[:-2]
        step = pl.program_id(0)
        turn, place = step // steps, step % steps

        @pl.when(step == 0)
        def _():
            for x in range(across_px):
                rows_of = slice(x * xb, (x + 1) * xb)
                for y in range(across_py):
                    for n, field in enumerate(which):
                        start = n * width + y * part
                        piece = arrived_ref[y, x, 0 if only else at_fields.index(field)]
                        lines[rows_of, start : start + part] = piece
                    if first:
                        piece = arrived_ref[y, x, at_fields.index(U)]
                        speed_ref[rows_of, y * part : (y + 1) * part] = piece

        block = op_ref[...].reshape(3 * many * rows, length)
        whole_result = jnp.dot(block, lines[...], preferred_element_type=jnp.float32)
        for n, field in enumerate(which):
            result = whole_result[:, n * width : (n + 1) * width].reshape(3, many, rows, width)
            for c in range(many):
                if first:
                    row = (place * many + c) * xb + (at[1] ^ turn) * rows
                    u = speed_ref[pl.ds(pl.multiple_of(row, rows), rows), :]
                else:
                    u = speed_ref[c, 0]
                value = result[2, c] + time_step * (
                    -u.astype(jnp.float32) * result[0, c] + visc_ref[field] * result[1, c]
                )
                value = value.astype(jnp.bfloat16)
                for r in range(members):

                    @pl.when(turn == r)
                    def _():
                        outs[n * members + r][c] = value

    def out_block(r):
        return pl.BlockSpec(
            (many, rows, width), lambda i, at: (jnp.clip(i - r * steps, 0, steps - 1), 0, 0)
        )

    def place_of(i, at):
        return i % steps, at[1] ^ (i // steps), 0, 0

    in_specs = [
        smem,
        pl.BlockSpec((3, many, 1, rows, length), lambda i, at: (0,) + place_of(i, at)),
        pl.BlockSpec(
            (across_py, across_px, 1 if only else held, xb, part),
            lambda i, at: (0, 0, at_fields.index(which[0]) if only else 0, 0, 0),
        ),
    ]
    args = [viscosity, operators.reshape(3, across_px, members, rows, length), arrived]
    out_specs = [out_block(r) for _ in which for r in range(members)]
    out_shape = [jax.ShapeDtypeStruct((across_px, rows, width), jnp.bfloat16)] * len(out_specs)
    if first:
        out_specs.append(whole((length, width)))
        out_shape.append(jax.ShapeDtypeStruct((length, width), jnp.bfloat16))
    else:
        in_specs.append(pl.BlockSpec((many, 1, rows, width), place_of))
        args.append(speed.reshape(across_px, members, rows, width))
    outs = chain.run(
        "x_pass",
        kernel,
        args,
        in_specs,
        out_specs,
        out_shape,
        grid=(steps * members,),
        scratch=[pltpu.VMEM((length, fields * width), jnp.bfloat16)],
        flops=6 * length * length * width * fields,
        limit=MOST_VMEM_BYTES,
    )
    return [outs[n * members : (n + 1) * members] for n in range(fields)], outs[-1] if first else speed


def y_pass(chain, which, operators, viscosity, parts, speed, yb, shape):
    across_px, rows, width = parts[0][0].shape
    fields, members = len(parts), len(parts[0])
    part = yb // members
    length = width * members
    blocks = length // yb
    height = across_px * rows
    first = which[0] == V

    def kernel(at, visc_ref, op_ref, *refs):
        part_refs, rest = refs[: fields * members], refs[fields * members :]
        if first:
            out, speed_ref, lines = rest
        else:
            speed_ref, out, mark, lines = rest
            mark[...] = jnp.zeros_like(mark)
        step = pl.program_id(0)

        @pl.when(step == 0)
        def _():
            for n in range(fields):
                for r in range(members):
                    values = part_refs[n * members + r][...].reshape(height, width)
                    if in_order(part):
                        for y in range(blocks):
                            start = pl.multiple_of(y * yb + (at[1] ^ r) * part, part)
                            lines[n, :, pl.ds(start, part)] = values[:, y * part : (y + 1) * part]
                    else:
                        start = pl.multiple_of((at[1] ^ r) * width, width)
                        lines[n, :, pl.ds(start, width)] = values
            if first:
                for y in range(blocks):
                    if in_order(part):
                        speed_ref[y] = lines[0, :, y * yb : (y + 1) * yb]
                    else:
                        for k in range(members):
                            start = k * width + y * part
                            speed_ref[y, :, k * part : (k + 1) * part] = lines[0, :, start : start + part]

        v = speed_ref[step if first else 0].astype(jnp.float32)
        whole_result = lax.dot_general(
            lines[...].reshape(fields * height, length),
            op_ref[...].reshape(3 * yb, length),
            (((1,), (1,)), ((), ())),
            preferred_element_type=jnp.float32,
        )
        for n, field in enumerate(which):
            result = whole_result[n * height : (n + 1) * height]
            value = result[:, 2 * yb :] + time_step * (
                -v * result[:, :yb] + visc_ref[field] * result[:, yb : 2 * yb]
            )
            value = value.astype(jnp.bfloat16)
            out[0, :, n] = value.reshape(across_px, rows, yb)

    flat = [part for field_parts in parts for part in field_parts]
    in_specs = [smem, pl.BlockSpec((3, yb, length), lambda i, at: (0, i, 0))] + like(flat)
    args = [viscosity, operators, *flat]
    out_specs = [pl.BlockSpec((1,) + shape[1:], lambda i, at: (i, 0, 0, 0, 0))]
    out_shape = [jax.ShapeDtypeStruct(shape, jnp.bfloat16)]
    if first:
        out_specs.append(whole((blocks, height, yb)))
        out_shape.append(jax.ShapeDtypeStruct((blocks, height, yb), jnp.bfloat16))
    else:
        in_specs.append(pl.BlockSpec((1, height, yb), lambda i, at: (i, 0, 0)))
        args.append(speed)
        out_specs.append(whole((8, 128)))
        out_shape.append(jax.ShapeDtypeStruct((8, 128), jnp.float32))
    outs = chain.run(
        "y_pass",
        kernel,
        args,
        in_specs,
        out_specs,
        out_shape,
        grid=(blocks,),
        scratch=[pltpu.VMEM((fields, height, length), jnp.bfloat16)],
        flops=6 * length * length * height * fields,
        limit=MOST_VMEM_BYTES,
    )
    return outs[0], outs[1] if first else speed


def put(chain, buffer, arrived, which, block, shape):
    across_py, across_px = arrived.shape[:2]
    extra = [] if buffer is None else [buffer]
    many = len(which)
    first, stride = which[0], which[1] - which[0] if many > 1 else 0

    def kernel(at, arrived_ref, *refs):
        refs[-1][...] = arrived_ref[...].reshape(refs[-1].shape)

    return chain.run(
        "put",
        kernel,
        [arrived, *extra],
        [pl.BlockSpec((across_py, across_px, block) + arrived.shape[3:], lambda n, at: (0, 0, n, 0, 0))]
        + [anywhere] * len(extra),
        [pl.BlockSpec((1,) + shape[1:], lambda n, at: (first + n * stride, 0, 0, 0))],
        [jax.ShapeDtypeStruct(shape, arrived.dtype)],
        grid=(many,),
        aliases={2: 0} if extra else {},
        limit=SMALL_VMEM_BYTES,
        free=True,
    )[0]


def wall_places(chain, tile, slot, span, slots):
    count = tile.shape[0]

    def kernel(at, tile_ref, slot_ref, chosen, filled):
        places = lax.broadcasted_iota(jnp.int32, (count, span), 1)
        chosen[...] = (tile_ref[...] == places).astype(jnp.float32).astype(jnp.bfloat16)
        places = lax.broadcasted_iota(jnp.int32, (slots, count), 0)
        filled[...] = (slot_ref[...] == places).astype(jnp.float32).astype(jnp.bfloat16)

    args = [tile.reshape(-1, 1), slot.reshape(1, -1)]
    shapes = [(count, span), (slots, count)]
    return chain.run(
        "wall_places",
        kernel,
        args,
        like(args),
        [whole(shape) for shape in shapes],
        [jax.ShapeDtypeStruct(shape, jnp.bfloat16) for shape in shapes],
        limit=SMALL_VMEM_BYTES,
    )


def wall_lines(chain, arrived, n, chosen, filled, unit):
    across_py, across_px, _, rows, yb = arrived.shape

    def kernel(at, chosen_ref, filled_ref, arrived_ref, *refs):
        outs, lines = refs[:-1], refs[-1]
        flux = jnp.dot(
            chosen_ref[...],
            arrived_ref[...].reshape(chosen.shape[1], yb),
            preferred_element_type=jnp.float32,
        )
        lines[...] = jnp.dot(
            filled_ref[...], flux.astype(jnp.bfloat16), preferred_element_type=jnp.float32
        ).reshape(lines.shape)
        for s in range(across_py):
            outs[s][...] = lines[at[2] ^ s].astype(jnp.bfloat16)

    shape = (across_px, unit, yb)
    return chain.run(
        "wall_lines",
        kernel,
        [chosen, filled, arrived],
        like([chosen, filled])
        + [pl.BlockSpec((across_py, across_px, 1, rows, yb), lambda i, at: (0, 0, n, 0, 0))],
        [whole(shape)] * across_py,
        [jax.ShapeDtypeStruct(shape, jnp.bfloat16)] * across_py,
        scratch=[pltpu.VMEM((across_py,) + shape, jnp.float32)],
        limit=SMALL_VMEM_BYTES,
    )


def wall_columns(chain, pieces):
    across_py, (across_px, unit, yb) = len(pieces), pieces[0].shape

    def kernel(at, *refs):
        outs = refs[across_py:]
        for t in range(across_px):
            for s in range(across_py):
                outs[t][at[2] ^ s] = refs[s][at[7] ^ t]

    shape = (across_py, unit, yb)
    return chain.run(
        "wall_columns",
        kernel,
        [*pieces],
        like(pieces),
        [whole(shape)] * across_px,
        [jax.ShapeDtypeStruct(shape, jnp.bfloat16)] * across_px,
        limit=SMALL_VMEM_BYTES,
    )


def add_flux(chain, tags, arrived, solid_temp, conductivity):
    rows, columns = solid_temp.shape
    across_px, (across_py, unit, _) = len(arrived), arrived[0].shape

    def kernel(at, temp_ref, kappa_ref, *refs):
        line_refs, tag_refs, out = refs[:across_px], refs[across_px:-1], refs[-1]
        out[0] = temp_ref[...]
        out[1] = kappa_ref[...]
        places = lax.broadcasted_iota(jnp.int32, (rows, unit), 0)
        source = jnp.zeros((rows, columns), jnp.float32)
        for s in range(across_py):
            chosen = [(tag_refs[s][t] == places).astype(jnp.float32) for t in range(across_px)]
            lines = [line_refs[t][at[2] ^ s] for t in range(across_px)]
            source = source + jnp.dot(
                jnp.concatenate(chosen, axis=1).astype(jnp.bfloat16),
                jnp.concatenate(lines, axis=0),
                preferred_element_type=jnp.float32,
            )
        out[2] = (wall_gain * source_gain) * source

    args = [solid_temp, conductivity, *arrived, *tags]
    return chain.run(
        "add_flux",
        kernel,
        args,
        like(args),
        [whole((3, rows, columns))],
        [jax.ShapeDtypeStruct((3, rows, columns), jnp.float32)],
        limit=SMALL_VMEM_BYTES,
    )[0]


def conduct(chain, solid, low, high, margin):
    kinds, height, columns = solid.shape
    rows = height - 2 * margin
    wide = columns + -(-2 * margin // 128) * 128

    def kernel(at, solid_ref, low_ref, high_ref, out, ext):
        ext[:, :, columns:] = jnp.zeros((kinds, height, wide - columns), jnp.float32)
        ext[:, :, :columns] = solid_ref[...]
        ext[:, :, columns : columns + margin] = high_ref[...]
        ext[:, :, wide - margin :] = low_ref[...]
        t, kappa, heat = ext[0], ext[1], ext[2]
        row = lax.broadcasted_iota(jnp.int32, (height, wide), 0) + at[3]
        col = lax.broadcasted_iota(jnp.int32, (height, wide), 1)
        col = jnp.where(col < wide - margin, col, col - wide) + at[4]
        inside = (row >= 0) & (row < at[5]) & (col >= 0) & (col < at[6])
        moves = ((height - 1, 0), (1, 0), (wide - 1, 1), (1, 1))
        faces = [
            jnp.where(inside, diffusion_rate * 0.5 * (kappa + pltpu.roll(kappa, shift, dim)), 0.0)
            for shift, dim in moves
        ]
        for _ in range(COND_STEPS):
            change = heat
            for face, (shift, dim) in zip(faces, moves):
                change = change + face * (pltpu.roll(t, shift, dim) - t)
            t = t + change
        out[...] = t[margin : margin + rows, :columns]

    args = [solid, low, high]
    return chain.run(
        "conduct",
        kernel,
        args,
        like(args),
        [whole((rows, columns))],
        [jax.ShapeDtypeStruct((rows, columns), jnp.float32)],
        scratch=[pltpu.VMEM((kinds, height, wide), jnp.float32)],
        limit=SMALL_VMEM_BYTES,
    )[0]


def on_device(
    fields,
    x_operators,
    y_operators,
    viscosity,
    wall_tile,
    wall_owner,
    wall_row,
    solid_temp,
    conductivity,
):
    across_px, across_py = lax.axis_size("px"), lax.axis_size("py")
    devices = across_px * across_py
    layers, xb, yb = fields.shape[1:]
    groups = layers // across_py
    members = across_px // groups
    a, b = lax.axis_index("px"), lax.axis_index("py")
    q, m = a // members, a % members
    rows, columns = solid_temp.shape
    margin = COND_STEPS
    at = jnp.stack(
        [
            q,
            m,
            b,
            a * rows - margin,
            b * columns,
            across_px * rows,
            across_py * columns,
            a,
        ]
    ).astype(jnp.int32)
    chain = Chain(at)

    def along(axis, pieces):
        return [pieces[0]] + [
            lax.ppermute(piece, axis, [(i, i ^ s) for i in range(lax.axis_size(axis))])
            for s, piece in enumerate(pieces[1:], 1)
        ]

    def exchange(blocks):
        moved = lax.all_to_all(
            blocks.reshape((devices,) + blocks.shape[2:]),
            ("py", "px"),
            split_axis=0,
            concat_axis=0,
            tiled=True,
        )
        return moved.reshape(blocks.shape)

    half, speeds = {}, {}

    def forward(*which):
        return exchange(cut(chain, fields, which, across_px, across_py))

    def X(arrived, at_fields, *which):
        outs, speeds[U] = x_pass(
            chain, which, x_operators, viscosity, arrived, at_fields, members, speeds.get(U)
        )
        for f, out in zip(which, outs):
            half[f] = along("px", out)

    y_columns = y_operators
    if not in_order(yb // members):
        y_columns = y_columns.reshape(3, -1, across_py, members, yb // members)
        y_columns = y_columns.swapaxes(2, 3).reshape(y_operators.shape)

    def Y(*which):
        shape = (across_py, across_px, len(which), xb // members, yb)
        out, speeds[V] = y_pass(
            chain,
            which,
            y_columns,
            viscosity,
            [half[f] for f in which],
            speeds.get(V),
            yb,
            shape,
        )
        return out

    most = forward(U, V, THETA)

    count = wall_tile.shape[0]
    owner = wall_owner[:, 0]
    unit = max(2, 4 * count // devices)
    order = jnp.arange(count, dtype=jnp.int32)
    earlier = (owner[:, None] == owner[None, :]) & (order[None, :] < order[:, None])
    position = jnp.sum(earlier.astype(jnp.int32), axis=1)
    label = owner * unit + position
    filled = label[None, :] == jnp.arange(devices * unit, dtype=jnp.int32)[:, None]
    labels = jnp.sum(jnp.where(filled, wall_row[None, :] + 1, 0), axis=1) - 1
    labels = labels.reshape(across_px, across_py, unit)
    slot = (owner % across_py * across_px + owner // across_py) * unit + position
    tags = along(
        "px",
        [lax.dynamic_index_in_dim(labels, a ^ s, 0, keepdims=False) for s in range(across_px)],
    )
    chain.last += tags
    last = forward(W)
    tags = along(
        "py",
        [
            jnp.stack([lax.dynamic_index_in_dim(tag, b ^ s, 0) for tag in tags])
            for s in range(across_py)
        ],
    )

    X(most, (U, V, THETA), V, THETA)
    first = exchange(Y(V, THETA))
    X(most, (U, V, THETA), U)
    X(last, (W,), W)
    second = Y(U, W)
    chosen, filled = wall_places(chain, wall_tile, slot, layers * xb, devices * unit)
    chain.last += tags
    flux = along("py", wall_lines(chain, first, 1, chosen, filled, unit))
    flux, second = lax.optimization_barrier((flux, second))
    second = exchange(second)
    flux = wall_columns(chain, flux)
    solid = add_flux(chain, tags, along("px", flux), solid_temp, conductivity)
    new_fields = put(chain, None, first, (V, THETA), 1, fields.shape)
    low, high = margins(solid, "px", 1, margin)
    solid = jnp.concatenate([low, solid, high], axis=1)
    low, high = margins(solid, "py", 2, margin)
    new_solid = conduct(chain, solid, low, high, margin)
    new_fields = put(chain, new_fields, second, (U, W), 1, fields.shape)
    return new_fields, new_solid


def solution(mesh):
    return jax.shard_map(
        on_device,
        mesh=mesh,
        in_specs=(
            P(None, None, "px", "py"),
            P(),
            P(),
            P(),
            P(("px", "py")),
            P(("px", "py"), None),
            P(("px", "py")),
            P("px", "py"),
            P("px", "py"),
        ),
        out_specs=(P(None, None, "px", "py"), P("px", "py")),
        check_vma=False,
    )
```
